32 devices in a mesh: fsdp: 8 (over z, x), tensor: 4 (over y, core).
Axes of the slice: x: 2, y: 2, z: 4, core: 2. Of those that a mesh axis runs over, the one named last changes fastest.
Arguments:
- tokens: bfloat16 [8, 2, 512, 2048], P('fsdp', None, 'tensor'), may hold values from -6 to 6
- lengths: int32 [8], P('fsdp'), may hold values from 512 to 1024, as said below
- w_query: bfloat16 [2048, 2048], P('fsdp', 'tensor'), may hold values from -0.5 to 0.5
- w_key: bfloat16 [2048, 512], P('fsdp', 'tensor'), may hold values from -0.5 to 0.5
- w_value: bfloat16 [2048, 512], P('fsdp', 'tensor'), may hold values from -0.125 to 0.125
- w_out: bfloat16 [2048, 2048], P('tensor', 'fsdp'), may hold values from -3 to 3
- w_gate: bfloat16 [2048, 8192], P('fsdp', 'tensor'), may hold values from -0.125 to 0.125
- w_up: bfloat16 [2048, 8192], P('fsdp', 'tensor'), may hold values from -0.125 to 0.125
- w_down: bfloat16 [8192, 2048], P('tensor', 'fsdp'), may hold values from -0.5 to 0.5
- gain_attn: bfloat16 [2048], P('fsdp'), may hold values from 0.5 to 1.5
- gain_mlp: bfloat16 [2048], P('fsdp'), may hold values from 0.5 to 1.5
- cotangent: bfloat16 [8, 2, 512, 2048], P('fsdp', None, 'tensor'), may hold values from -6 to 6
Outputs:
- output: float32 [8, 2, 512, 2048], P('fsdp', None, 'tensor')
- input_grad: float32 [8, 2, 512, 2048], P('fsdp', None, 'tensor')
- grad_query: float32 [2048, 2048], P('fsdp', 'tensor')
- grad_key: float32 [2048, 512], P('fsdp', 'tensor')
- grad_value: float32 [2048, 512], P('fsdp', 'tensor')
- grad_out: float32 [2048, 2048], P('tensor', 'fsdp')
- grad_gate: float32 [2048, 8192], P('fsdp', 'tensor')
- grad_up: float32 [2048, 8192], P('fsdp', 'tensor')
- grad_down: float32 [8192, 2048], P('tensor', 'fsdp')
- grad_gain_attn: float32 [2048], P(('fsdp', 'tensor'))
- grad_gain_mlp: float32 [2048], P(('fsdp', 'tensor'))
The draws below stay inside these ranges and needn't reach their ends.
Inputs may be any that keep to these rules, and one draw needn't show every extreme that they name: `lengths`: valid slots of each sequence; some sequence has all 1024 slots valid.
All inputs are finite; a program needn't handle non-finite values.
Results may differ from the reference program's by a relative error of at most 0.019.
Values may be sent and summed in bfloat16 or wider, within the bound.
No kernel may reach another device: no remote copies, remote signals or barrier semaphores. Data moves between devices by JAX's collectives and lax.ppermute only.
A program may use at most 256 MiB of HBM per device.

```python
import jax
import jax.numpy as jnp
from jax import lax

D = 2048
HEADS = 32
KV_HEADS = 8
HEAD_DIM = 64
FF = 8192
QROWS = 512
MICRO = 2
LENGTH = 1024
SEQS = 8


def draw_lengths(key, part):
    key = jax.random.fold_in(key, 11)
    first_key, second_key = jax.random.split(key)
    drawn = jax.random.randint(first_key, (SEQS,), LENGTH // 2, LENGTH + 1)
    longest = jax.random.randint(second_key, (), 0, SEQS)
    return jnp.where(jnp.arange(SEQS) == longest, LENGTH, drawn).astype(jnp.int32)


def block_levels(key, extent, cuts, least, high):
    factor_of = 1.0
    for dim, shards_of in cuts:
        draws = jax.random.uniform(jax.random.fold_in(jax.random.fold_in(key, 6), dim), (shards_of,), jnp.float32, least / len(cuts), high / len(cuts))
        factor_of = factor_of * jnp.repeat(jnp.exp(draws), extent[dim] // shards_of).reshape((-1,) + (1,) * (len(extent) - 1 - dim))
    return factor_of


def gaussian(stream_key, extent, spread, limit, cuts=(), dtype=jnp.bfloat16):
    loudness = block_levels(stream_key, extent, cuts, -0.22, 0.18) if cuts else 1.0
    array = jax.random.normal(stream_key, extent, jnp.float32) * spread * loudness
    return jnp.minimum(jnp.maximum(array, -limit), limit).astype(dtype)


def setup_inputs(seed: int = 0) -> dict:
    key_of = jax.random.split(jax.random.key(seed), 13)
    return {
        "tokens": gaussian(key_of[0], (SEQS, MICRO, QROWS, D), 1.0, 6.0, ((0, 8), (2, 4))),
        "lengths": draw_lengths(jax.random.fold_in(key_of[12], 71), 0),
        "w_query": gaussian(key_of[2], (D, D), (D // 16) ** -0.5, 0.5, ((0, 8), (1, 4))),
        "w_key": gaussian(key_of[3], (D, KV_HEADS * HEAD_DIM), (D // 16) ** -0.5, 0.5, ((0, 8), (1, 4))),
        "w_value": gaussian(key_of[4], (D, KV_HEADS * HEAD_DIM), D ** -0.5, 0.125, ((0, 8), (1, 4))),
        "w_out": gaussian(key_of[5], (D, D), (max(D // 512, 1)) ** -0.5, 3.0, ((0, 4), (1, 8))),
        "w_gate": gaussian(key_of[6], (D, FF), D ** -0.5, 0.125, ((0, 8), (1, 4))),
        "w_up": gaussian(key_of[7], (D, FF), D ** -0.5, 0.125, ((0, 8), (1, 4))),
        "w_down": gaussian(key_of[8], (FF, D), (FF // 64) ** -0.5, 0.5, ((0, 4), (1, 8))),
        "gain_attn": jnp.clip(1.0 + 0.1 * jax.random.normal(key_of[9], (D,), jnp.float32), 0.5, 1.5).astype(jnp.bfloat16),
        "gain_mlp": jnp.clip(1.0 + 0.1 * jax.random.normal(key_of[10], (D,), jnp.float32), 0.5, 1.5).astype(jnp.bfloat16),
        "cotangent": gaussian(key_of[11], (SEQS, MICRO, QROWS, D), 1.0, 6.0, ((0, 8), (2, 4))),
    }


EPS = 1e-05
MULT = 0.015625
RESIDUAL = 0.22
THETA = 10000000.0
NEGATIVE = -1e+30
HIGH = lax.Precision.HIGHEST

@jax.custom_vjp
def low(v):
    return lax.optimization_barrier(v.astype(jnp.bfloat16)).astype(jnp.float32)

@jax.custom_vjp
def low_back(v):
    return v

def low_keep(v):
    return (low(v), None)

def low_pass(kept, grad):
    return (grad,)

def back_keep(v):
    return (v, None)

def back_low(kept, grad):
    return (low(grad),)
low.defvjp(low_keep, low_pass)
low_back.defvjp(back_keep, back_low)

def normalize(values, gain):
    factor = lax.rsqrt(lax.optimization_barrier(jnp.mean(values * values, -1, keepdims=True)) + EPS)
    return values * factor * gain

def rope_tables(positions, half):
    freqs = jnp.exp(-jnp.log(THETA) * jnp.arange(half).astype(jnp.float32) / half)
    angles = positions[:, None] * freqs[None, :]
    return (jnp.cos(angles)[:, None, :], jnp.sin(angles)[:, None, :])

def rotate(values, cosines, sines):
    half = values.shape[-1] // 2
    first = values[..., :half]
    second = values[..., half:]
    return jnp.concatenate([first * cosines - second * sines, second * cosines + first * sines], -1)

def forward(stream, length, w_query, w_key, w_value, w_out, w_gate, w_up, w_down, gain_attn, gain_mlp):
    positions = jnp.arange(LENGTH)
    cosines, sines = rope_tables(positions.astype(jnp.float32), HEAD_DIM // 2)
    normed = low(normalize(stream, gain_attn))
    queries = low_back(jnp.dot(normed, w_query, precision=HIGH)).reshape(LENGTH, HEADS, HEAD_DIM)
    queries = low(rotate(queries, cosines, sines))
    keys = low_back(jnp.dot(normed, w_key, precision=HIGH)).reshape(LENGTH, KV_HEADS, HEAD_DIM)
    keys = low(rotate(keys, cosines, sines))
    values = low(low_back(jnp.dot(normed, w_value, precision=HIGH))).reshape(LENGTH, KV_HEADS, HEAD_DIM)
    grouped = queries.reshape(LENGTH, KV_HEADS, HEADS // KV_HEADS, HEAD_DIM)
    scores = low_back(MULT * jnp.einsum('qgrd,kgd->grqk', grouped, keys, precision=HIGH))
    allowed = (positions[None, :] <= positions[:, None]) & (positions[None, :] < length)
    scores = jnp.where(allowed, scores, NEGATIVE)
    top = lax.optimization_barrier(jnp.max(scores, -1, keepdims=True))
    expd = jnp.exp(scores - top)
    probs = expd / lax.optimization_barrier(jnp.sum(expd, -1, keepdims=True))
    mixed = jnp.einsum('grqk,kgd->qgrd', low(probs), values, precision=HIGH).reshape(LENGTH, HEADS * HEAD_DIM)
    mixed = low(low_back(mixed))
    attended = low_back(jnp.dot(mixed, w_out, precision=HIGH))
    middle = stream + RESIDUAL * attended
    second = low(normalize(middle, gain_mlp))
    gate = low_back(jnp.dot(second, w_gate, precision=HIGH))
    up = low_back(jnp.dot(second, w_up, precision=HIGH))
    hidden = low(jax.nn.silu(gate) * up)
    branch = low_back(jnp.dot(hidden, w_down, precision=HIGH))
    valid = (positions < length).astype(jnp.float32)[:, None]
    return valid * (middle + RESIDUAL * branch)

def reference(tokens, lengths, w_query, w_key, w_value, w_out, w_gate, w_up, w_down, gain_attn, gain_mlp, cotangent):
    weights = (w_query.astype(jnp.float32), w_key.astype(jnp.float32), w_value.astype(jnp.float32), w_out.astype(jnp.float32), w_gate.astype(jnp.float32), w_up.astype(jnp.float32), w_down.astype(jnp.float32), gain_attn.astype(jnp.float32), gain_mlp.astype(jnp.float32))
    streams = tokens.astype(jnp.float32).reshape(SEQS, LENGTH, D)
    pulls = cotangent.astype(jnp.float32).reshape(SEQS, LENGTH, D)

    def one_sequence(carry, item):
        stream, length, upstream = item

        def apply_layer(values, *params):
            return forward(values, length, *params)
        result, pull = jax.vjp(apply_layer, stream, *weights)
        grads = pull(upstream)
        summed = tuple((total + part for total, part in zip(carry, grads[1:])))
        return (summed, (result, grads[0]))
    start = tuple((jnp.zeros_like(weight) for weight in weights))
    totals, (results, stream_grads) = lax.scan(one_sequence, start, (streams, lengths, pulls))
    return (results.reshape(tokens.shape), stream_grads.reshape(tokens.shape), totals[0], totals[1], totals[2], totals[3], totals[4], totals[5], totals[6], totals[7], totals[8])
```

```python
import functools

import jax
import jax.numpy as jnp
from jax import lax
from jax.experimental import pallas as pl
from jax.experimental.pallas import tpu as pltpu
from jax.sharding import Mesh, PartitionSpec as P

HEAD_DIM = 64
EPS = 1e-05
MULT = 0.015625
RESIDUAL = 0.22
THETA = 10000000.0
NEGATIVE = -1e30
F32 = jnp.float32
BF16 = jnp.bfloat16
BLOCK = 256
VMEM_LIMIT = 56 * 1024 * 1024
SMEM = pltpu.SMEM


def nn(a, b):
    return lax.dot_general(a, b, (((1,), (0,)), ((), ())), preferred_element_type=F32)


def nt(a, b):
    return lax.dot_general(a, b, (((1,), (1,)), ((), ())), preferred_element_type=F32)


def tn(a, b):
    return lax.dot_general(a, b, (((0,), (0,)), ((), ())), preferred_element_type=F32)


def params():
    return pltpu.CompilerParams(vmem_limit_bytes=VMEM_LIMIT)


def hops(sources, place):
    pairs = []
    for x in range(2):
        for y in range(2):
            for c in range(2):
                if sources != ("same" if x == c else "other"):
                    continue
                px, py, pc = place(x, y, c)
                pairs.append((x * 4 + y * 2 + c, px * 4 + py * 2 + pc))
    return pairs


def over_x(x, y, c):
    return 1 - x, y, c


def over_y(x, y, c):
    return x, 1 - y, c


def over_core(x, y, c):
    return x, y, 1 - c


def flip(pairs):
    return [pair[::-1] for pair in pairs]


FIRST = hops("other", lambda x, y, c: (c, y, x)) + hops("same", over_y)
SECOND = hops("same", over_x) + hops("other", lambda x, y, c: (x, 1 - y, 1 - c))
THIRD = hops("other", over_core)
PASS_Y = hops("other", over_y)
PASS_X = hops("same", over_x)


def send(values, pairs):
    return lax.ppermute(values, ("lo", "y", "core"), pairs)


def trade(values):
    received = send(values, hops("other", lambda x, y, c: (c, y, x)))
    return jnp.where(is_same(), values, received)


def is_same():
    return lax.axis_index("lo") == lax.axis_index("core")


def after(value, anchor):
    return lax.optimization_barrier((value, anchor))[0]


def send_rows(piece):
    first = send(piece, FIRST)
    second = send(piece, SECOND)
    third = send(piece, THIRD)
    return [first, second, third, send(first, PASS_Y), piece, send(first, PASS_X)]


def assemble_kernel(starts, *refs):
    pieces, out, sems = refs[:6], refs[6], refs[7]
    rows = pieces[0].shape[0]

    def copy(piece, k):
        start = pl.multiple_of(starts[k], rows)
        return pltpu.make_async_copy(pieces[piece], out.at[pl.ds(start, rows)], sems.at[k])

    copy(0, 0).start()
    copy(1, 1).start()

    @pl.when(starts[4] == 1)
    def _():
        copy(2, 2).start()
        copy(4, 3).start()

    @pl.when(starts[4] != 1)
    def _():
        copy(3, 2).start()
        copy(5, 3).start()

    for k in range(4):
        copy(k, k).wait()


def join_rows(pieces, starts):
    rows, width = pieces[0].shape
    return pl.pallas_call(
        assemble_kernel,
        out_shape=jax.ShapeDtypeStruct((4 * rows, width), pieces[0].dtype),
        in_specs=[pl.BlockSpec(memory_space=SMEM)] + [pl.BlockSpec(memory_space=pl.ANY)] * 6,
        out_specs=pl.BlockSpec(memory_space=pltpu.VMEM),
        scratch_shapes=[pltpu.SemaphoreType.DMA((4,))],
        compiler_params=params(),
        name="assemble",
    )(starts, *pieces)


def send_sums(parts):
    across_y = send(parts[2], flip(PASS_Y))
    across_x = send(parts[3], flip(PASS_X))
    second = send(parts[1], flip(SECOND))
    third = send(parts[2], flip(THIRD))
    passed = jnp.where(is_same(), across_x, across_y).astype(F32)
    first = send((parts[0].astype(F32) + passed).astype(BF16), flip(FIRST))
    return [first, second, jnp.where(is_same(), parts[3], third)]


def add_sums(parts):
    return sum(part.astype(F32) for part in parts)


def swap_z(values, step, count):
    return lax.ppermute(values, "hi", [(i, i ^ step) for i in range(count)])


class Order:

    def __init__(self):
        self.last = None

    def __call__(self, step, first, *rest):
        if self.last is not None:
            first = after(first, self.last)
        found = step(first, *rest)
        self.last = jax.tree.leaves(found)[0]
        return found


def project_kernel(pairs, rows, starts, *refs):
    lhs, rhs = refs[:pairs], refs[pairs : 2 * pairs]
    outs, total = refs[2 * pairs : -1], refs[-1]
    value = None
    for a, b in zip(lhs, rhs):
        term = nt(a[...], b[...])
        value = term if value is None else value + term
    total[...] = value
    for k, out in enumerate(outs):
        start = pl.multiple_of(starts[k], rows)
        out[...] = total[pl.ds(start, rows), :].astype(BF16)


def project(starts, lhs, rhs, places):
    tall = lhs[0].shape[0]
    count = 4
    rows = tall // count
    wide = rhs[0].shape[0]
    step = min(512, wide)

    def still(j):
        return (0, 0)

    def columns(size, place):
        return pl.BlockSpec((step, size), lambda j: (j, place))

    return pl.pallas_call(
        functools.partial(project_kernel, len(lhs), rows),
        grid=(wide // step,),
        out_shape=(jax.ShapeDtypeStruct((rows, wide), BF16),) * count,
        in_specs=[pl.BlockSpec(memory_space=SMEM)]
        + [pl.BlockSpec(a.shape, still) for a in lhs]
        + [columns(a.shape[1], place) for a, place in zip(lhs, places)],
        out_specs=(pl.BlockSpec((rows, step), lambda j: (0, j)),) * count,
        scratch_shapes=[pltpu.VMEM((tall, step), F32)],
        compiler_params=params(),
        name="project",
    )(starts, *lhs, *rhs)


def mlp_kernel(count, *refs):
    seconds, branch_grads = refs[:count], refs[count : 2 * count]
    w_gate, w_up, w_down = refs[2 * count : 2 * count + 3]
    outs = refs[2 * count + 3 :]
    for m in range(count):
        hidden, gate_back, up_back = outs[3 * m : 3 * m + 3]
        seen = seconds[m][...]
        gate = nn(seen, w_gate[...])
        up = nn(seen, w_up[...])
        grad = nn(branch_grads[m][...], w_down[...])
        sigma = 1.0 / (1.0 + jnp.exp(-gate))
        silu = gate * sigma
        hidden[...] = (silu * up).astype(BF16)
        up_back[...] = (grad * silu).astype(BF16)
        gate_back[...] = (grad * up * (sigma + silu * (1.0 - sigma))).astype(BF16)


def mlp(seconds, branch_grads, weight):
    count = len(seconds)
    tall, width = seconds[0].shape
    units = weight.shape[1] // 3
    step = min(256, units)
    steps = units // step
    whole = pl.BlockSpec((tall, width), lambda j: (0, 0), pipeline_mode=pl.Buffered(1))
    part = pl.BlockSpec((tall, step), lambda j: (0, j))
    shape = jax.ShapeDtypeStruct((tall, units), BF16)
    return pl.pallas_call(
        functools.partial(mlp_kernel, count),
        grid=(steps,),
        out_shape=(shape,) * (3 * count),
        in_specs=[whole] * (2 * count)
        + [
            pl.BlockSpec((width, step), lambda j, k=k: (0, k * steps + j)) for k in range(3)
        ],
        out_specs=(part,) * (3 * count),
        compiler_params=params(),
        name="mlp",
    )(*seconds, *branch_grads, weight, weight, weight)


def grads_kernel(plan, *refs):
    out = refs[-1]
    start = 0
    for pairs in plan:
        value = None
        for a, b in pairs:
            term = tn(refs[a][...], refs[b][...])
            value = term if value is None else value + term
        value = value.astype(BF16).reshape(out.shape[0], out.shape[1], value.shape[1])
        out[:, :, start : start + value.shape[2]] = value
        start += value.shape[2]


def weight_grads(products, count):
    arrays = []
    specs = []
    plan = []
    side = 0
    slab = products[0][0][0].shape[1] // count
    step = max(slab, 256)

    def place(array, cut):
        for i, known in enumerate(arrays):
            if known is array:
                return i
        tall, wide = array.shape
        if cut:
            specs.append(pl.BlockSpec((tall, step), lambda j: (0, j)))
        else:
            specs.append(
                pl.BlockSpec((tall, wide), lambda j: (0, 0), pipeline_mode=pl.Buffered(1))
            )
        arrays.append(array)
        return len(arrays) - 1

    for lhs, rhs in products:
        plan.append([(place(a, True), place(b, False)) for a, b in zip(lhs, rhs)])
        side += rhs[0].shape[1]
    return pl.pallas_call(
        functools.partial(grads_kernel, plan),
        grid=(count * slab // step,),
        out_shape=jax.ShapeDtypeStruct((count, slab, side), BF16),
        in_specs=specs,
        out_specs=pl.BlockSpec((step // slab, slab, side), lambda j: (j, 0, 0)),
        compiler_params=params(),
        name="grads",
    )(*arrays)


def turn(values, cosines, sines):
    lane = lax.broadcasted_iota(jnp.int32, values.shape, 1)
    other = jnp.where(
        lane % HEAD_DIM < HEAD_DIM // 2,
        pltpu.roll(values, 128 - HEAD_DIM // 2, 1),
        pltpu.roll(values, HEAD_DIM // 2, 1),
    )
    return values * cosines + other * sines


def head_block(values, head, high):
    tile = values[:, (head // 2) * 128 : (head // 2 + 1) * 128]
    if (head % 2 == 1) != high:
        tile = pltpu.roll(tile, HEAD_DIM, 1)
    lane = lax.broadcasted_iota(jnp.int32, tile.shape, 1)
    inside = (lane >= HEAD_DIM) if high else (lane < HEAD_DIM)
    return jnp.where(inside, tile, 0.0)


def bias_of(m, rows, j, length):
    seen = m * rows + (j + 1) * BLOCK
    first = m * rows if m else seen - BLOCK
    key = first + lax.broadcasted_iota(jnp.int32, (seen - first, BLOCK), 0)
    query = m * rows + j * BLOCK + lax.broadcasted_iota(jnp.int32, (seen - first, BLOCK), 1)
    return first, seen, jnp.where((key <= query) & (key < length), 0.0, NEGATIVE)


def scores_of(keys, query, bias, first, seen):
    scores = nt(keys[:seen], query)
    if first == 0:
        return scores + bias
    return jnp.concatenate([scores[:first], scores[first:] + bias], 0)


def forward_kernel(m, heads, lengths, *refs):
    tokens, weight, cos_q, sin_q, cos_k, sin_k = refs[:6]
    refs = refs[6:]
    if m:
        before, refs = refs[0], refs[1:]
    queries, pairs, log_total, mixed, factors, flipped = refs
    rows = tokens.shape[0]
    length = lengths[0]
    wide = tokens[...].astype(F32)
    factor = lax.rsqrt(jnp.mean(wide * wide, -1, keepdims=True) + EPS)
    factors[...] = jnp.broadcast_to(factor, (rows, 128))
    qkv = nn(tokens[...], weight[...]) * factor
    parts = []
    for i in range(heads // 2):
        parts.append(turn(qkv[:, i * 128 : (i + 1) * 128], cos_q[...], sin_q[...]))
    query = jnp.concatenate(parts, 1).astype(BF16).astype(F32) * MULT
    queries[...] = query.astype(BF16)
    pair = turn(qkv[:, heads * HEAD_DIM :], cos_k[...], sin_k[...]).astype(BF16)
    pairs[...] = pair
    if m:
        pair = jnp.concatenate([before[...], pair], 0)
    upright = jnp.transpose(pair.astype(F32)).astype(BF16)[HEAD_DIM:]
    for j in range(rows // BLOCK):
        first, seen, bias = bias_of(m, rows, j, length)
        here = slice(j * BLOCK, (j + 1) * BLOCK)
        for h in range(heads):
            q = head_block(query[here], h, False).astype(BF16)
            scores = scores_of(pair, q, bias, first, seen)
            top = jnp.max(scores, 0, keepdims=True)
            expd = jnp.exp(scores - top)
            total = jnp.sum(expd, 0, keepdims=True)
            log_total[0, h : h + 1, here] = top + jnp.log(total)
            out = nn(upright[:, :seen], expd.astype(BF16)) / total
            flipped[h * HEAD_DIM : (h + 1) * HEAD_DIM, here] = out
    mixed[...] = jnp.transpose(flipped[...]).astype(BF16)


def attend(m, heads, lengths, tokens, weight, tables, before):
    rows, width = tokens.shape
    q_width = heads * HEAD_DIM
    groups = weight.shape[1] // (2 * q_width + 128)

    def block(lanes):
        return pl.BlockSpec((rows, lanes), lambda g: (0, g))

    def whole(lanes, place=0):
        return pl.BlockSpec((rows, lanes), lambda g: (place, 0))

    return pl.pallas_call(
        functools.partial(forward_kernel, m, heads),
        grid=(groups,),
        out_shape=(
            jax.ShapeDtypeStruct((rows, groups * q_width), BF16),
            jax.ShapeDtypeStruct((rows, groups * 128), BF16),
            jax.ShapeDtypeStruct((groups, heads, rows), F32),
            jax.ShapeDtypeStruct((rows, groups * q_width), BF16),
            jax.ShapeDtypeStruct((rows, 128), F32),
        ),
        in_specs=[
            pl.BlockSpec(memory_space=SMEM),
            whole(width),
            pl.BlockSpec((width, q_width + 128), lambda g: (0, g)),
        ]
        + [whole(128, m)] * 4
        + ([block(128)] if m else []),
        out_specs=(
            block(q_width),
            block(128),
            pl.BlockSpec((1, heads, rows), lambda g: (g, 0, 0)),
            block(q_width),
            whole(128),
        ),
        scratch_shapes=[pltpu.VMEM((q_width, rows), F32)],
        compiler_params=params(),
        name="attend",
    )(lengths, tokens, weight, *tables, *([before] if m else []))


def backward_kernel(m, heads, last, lengths, *refs):
    grad, w_out, queries, pairs, log_total, factors = refs[:6]
    cos_q, sin_q, cos_k, sin_k = refs[6:10]
    refs = refs[10:]
    if m:
        before, refs = refs[0], refs[1:]
    if not last:
        later, refs = refs[0], refs[1:]
    back, scaled_back, refs = refs[0], refs[1], refs[2:]
    if m:
        earlier, refs = refs[0], refs[1:]
    flipped, pair_grad = refs
    rows = grad.shape[0]
    q_width = heads * HEAD_DIM
    length = lengths[0]
    mixed_grad = nn(grad[...], w_out[...]).astype(BF16).astype(F32)
    query = queries[...].astype(F32)
    pair = pairs[...]
    if m:
        pair = jnp.concatenate([before[...], pair], 0)
    upright = jnp.transpose(pair.astype(F32)).astype(BF16)[:HEAD_DIM]
    pair_grad[...] = jnp.zeros_like(pair_grad)
    if not last:
        pair_grad[m * rows :, :] = later[...]
    for j in range(rows // BLOCK):
        first, seen, bias = bias_of(m, rows, j, length)
        here = slice(j * BLOCK, (j + 1) * BLOCK)
        for h in range(heads):
            q = head_block(query[here], h, False).astype(BF16)
            g = head_block(mixed_grad[here], h, True).astype(BF16)
            scores = scores_of(pair, q, bias, first, seen)
            probs = jnp.exp(scores - log_total[0, h : h + 1, here])
            prob_grad = nt(pair[:seen], g)
            inner = jnp.sum(probs * prob_grad, 0, keepdims=True)
            score_grad = (probs * (prob_grad - inner)).astype(BF16)
            pair_grad[:seen, :] += nn(score_grad, q) + nn(probs.astype(BF16), g)
            flipped[h * HEAD_DIM : (h + 1) * HEAD_DIM, here] = nn(upright[:, :seen], score_grad)
    query_grad = jnp.transpose(flipped[...]) * MULT
    parts = []
    for i in range(heads // 2):
        parts.append(turn(query_grad[:, i * 128 : (i + 1) * 128], cos_q[...], -sin_q[...]))
    parts.append(turn(pair_grad[m * rows :, :], cos_k[...], -sin_k[...]))
    found = jnp.concatenate(parts, 1).astype(BF16)
    back[...] = found
    scaled_back[...] = (found.astype(F32) * factors[:, :1]).astype(BF16)
    if m:
        earlier[...] = pair_grad[: m * rows, :]


def attend_back(m, heads, last, lengths, grad, weight, kept, tables, before, later):
    rows, width = grad.shape
    q_width = heads * HEAD_DIM
    side = q_width + 128
    queries, pairs, log_total, factors = kept
    groups = queries.shape[1] // q_width
    first = groups * side // q_width

    def block(lanes):
        return pl.BlockSpec((rows, lanes), lambda g: (0, g))

    def whole(lanes, place=0):
        return pl.BlockSpec((rows, lanes), lambda g: (place, 0))

    back = jax.ShapeDtypeStruct((rows, groups * side), BF16)
    earlier = (jax.ShapeDtypeStruct((rows, groups * 128), F32),) if m else ()
    return pl.pallas_call(
        functools.partial(backward_kernel, m, heads, last),
        grid=(groups,),
        out_shape=(back, back) + earlier,
        in_specs=[
            pl.BlockSpec(memory_space=SMEM),
            whole(width),
            pl.BlockSpec((width, q_width), lambda g: (0, first + g)),
            block(q_width),
            block(128),
            pl.BlockSpec((1, heads, rows), lambda g: (g, 0, 0)),
            whole(128),
        ]
        + [whole(128, m)] * 4
        + ([block(128)] if m else [])
        + ([] if last else [block(128)]),
        out_specs=(block(side),) * 2 + ((block(128),) if m else ()),
        scratch_shapes=[
            pltpu.VMEM((q_width, rows), F32),
            pltpu.VMEM(((m + 1) * rows, 128), F32),
        ],
        compiler_params=params(),
        name="attend_back",
    )(
        lengths,
        grad,
        weight,
        queries,
        pairs,
        log_total,
        factors,
        *tables,
        *([before] if m else []),
        *([] if last else [later]),
    )


def norm_back(values, factor, weighted):
    scaled = values * factor
    product = weighted * scaled
    back = factor * (weighted - scaled * jnp.mean(product, -1, keepdims=True))
    return back, jnp.sum(product, 0)


def shards(
    tokens,
    lengths,
    w_query,
    w_key,
    w_value,
    w_out,
    w_gate,
    w_up,
    w_down,
    gain_attn,
    gain_mlp,
    cotangent,
):
    hi_count = lax.axis_size("hi")
    slabs = hi_count * 2
    z = lax.axis_index("hi")
    x = lax.axis_index("lo")
    y = lax.axis_index("y")
    c = lax.axis_index("core")
    t = y * 2 + c
    micro_count = tokens.shape[1]
    rows = tokens.shape[2]
    query_rows = rows * 4
    total_rows = micro_count * query_rows
    depth = w_query.shape[0]
    width = depth * slabs
    groups = w_key.shape[1] // HEAD_DIM
    heads = w_query.shape[1] // HEAD_DIM // groups
    q_width = heads * HEAD_DIM
    side = q_width + 128
    attn_column = gain_attn.astype(F32)[:, None]
    mlp_column = gain_mlp.astype(F32)[:, None]

    near = [y * 2 + x, y * 2 + 1 - x]
    far = [(1 - y) * 2 + x, (1 - y) * 2 + 1 - x]
    same = (x == c).astype(jnp.int32)
    starts = jnp.where(
        x == c,
        jnp.stack([far[0], far[1], near[1], near[0]]),
        jnp.stack([near[0], near[1], far[0], far[1]]),
    )
    starts = jnp.append(starts * rows, same).astype(jnp.int32)
    length = lengths[0]
    work_length = trade(lengths)

    order = Order()

    def gather_z(piece):
        return lax.all_gather(piece, ("hi", "core"), axis=0, tiled=True)

    def collect_z(products):
        lhs, rhs = products[0]

        def run(first):
            return weight_grads([(lhs, [first] + list(rhs[1:]))] + products[1:], slabs)

        total = order(run, rhs[0])
        return lax.psum_scatter(total, ("hi", "core"), scatter_dimension=0, tiled=False)

    def scaled(weight, column):
        return (weight.astype(F32) * column).astype(BF16)

    out_turned = jnp.transpose(w_out)
    down_turned = jnp.transpose(w_down)

    def attention_columns():
        parts = []
        for g in range(groups):
            parts.append(w_query[:, g * q_width : (g + 1) * q_width])
            parts.append(w_key[:, g * HEAD_DIM : (g + 1) * HEAD_DIM])
            parts.append(w_value[:, g * HEAD_DIM : (g + 1) * HEAD_DIM])
        return jnp.concatenate([scaled(jnp.concatenate(parts, 1), attn_column), out_turned], 1)

    def unit_columns(h):
        n = w_gate.shape[1] // 2
        here = slice(h * n, (h + 1) * n)
        return jnp.concatenate(
            [
                scaled(w_gate[:, here], mlp_column),
                scaled(w_up[:, here], mlp_column),
                down_turned[:, here],
            ],
            1,
        )

    half_dim = HEAD_DIM // 2
    freqs = jnp.exp(-jnp.log(THETA) * jnp.arange(half_dim).astype(F32) / half_dim)
    angles = jnp.arange(total_rows).astype(F32)[:, None] * freqs[None, :]
    cosines, sines = jnp.cos(angles), jnp.sin(angles)
    cos_head = jnp.concatenate([cosines, cosines], 1)
    sin_head = jnp.concatenate([-sines, sines], 1)
    tables = (
        jnp.concatenate([cos_head, cos_head], 1),
        jnp.concatenate([sin_head, sin_head], 1),
        jnp.concatenate([cos_head, jnp.ones_like(cos_head)], 1),
        jnp.concatenate([sin_head, jnp.zeros_like(sin_head)], 1),
    )

    valids = []
    upstreams = []
    streams = []
    attn_factors = []
    for m in range(micro_count):
        place = m * query_rows + t * rows + jnp.arange(rows)
        valid = (place < length).astype(F32)[:, None]
        valids.append(valid)
        upstreams.append(valid * cotangent[0, m].astype(F32))
        stream = tokens[0, m].astype(F32)
        streams.append(stream)
        attn_factors.append(lax.rsqrt(jnp.mean(stream * stream, -1, keepdims=True) + EPS))

    attn_piece = trade(after(attention_columns(), work_length))
    attn_weight = gather_z(attn_piece)
    here = [send_rows(after(tokens[0, 0], attn_piece))]
    units_piece = [trade(after(unit_columns(0), attn_piece))]
    tokens_all = [order(join_rows, here[0], starts)]
    here.append(send_rows(after(tokens[0, 1], attn_piece)))
    units_weight = [gather_z(order(lambda a: a, units_piece[0]))]

    def forward(m, rows_all):
        return attend(
            m, heads, work_length, rows_all, attn_weight, tables, found[0][1] if m else None
        )

    out_columns = attn_weight[:, groups * side :]

    def out_project(mixed):
        return project(starts, [mixed], [out_columns], [0])

    def enter(m, parts):
        middle = streams[m] + RESIDUAL * add_sums(parts)
        factor = lax.rsqrt(jnp.mean(middle * middle, -1, keepdims=True) + EPS)
        return (middle * factor).astype(BF16), middle, factor

    found = [order(lambda a: forward(0, a), tokens_all[0])]
    sums = [send_sums(order(out_project, found[0][3]))]
    tokens_all.append(order(join_rows, here[1], starts))
    branch_rows = [(RESIDUAL * upstreams[m]).astype(BF16) for m in range(micro_count)]
    branch = [send_rows(after(branch_rows[0], tokens_all[0]))]
    branch.append(send_rows(after(branch_rows[1], found[0][0])))
    branch_grads = [order(join_rows, branch[0], starts)]
    units_piece.append(trade(after(unit_columns(1), found[0][0])))
    found.append(order(lambda a: forward(1, a), tokens_all[1]))
    sums.append(send_sums(order(out_project, found[1][3])))
    entered = [order(lambda a: enter(0, a), sums[0])]
    here = [send_rows(entered[0][0])]
    branch_grads.append(order(join_rows, branch[1], starts))
    units_weight.append(gather_z(order(lambda a: a, units_piece[1])))
    second_all = [order(join_rows, here[0], starts)]
    entered.append(order(lambda a: enter(1, a), sums[1]))
    here.append(send_rows(entered[1][0]))
    second_all.append(order(join_rows, here[1], starts))
    middles = [e[1] for e in entered]
    mlp_factors = [e[2] for e in entered]

    hiddens, gate_backs, up_backs, unit_grads = [], [], [], []
    def back_project(m):
        def run(first):
            return project(
                starts,
                [first, up_backs[0][m], gate_backs[1][m], up_backs[1][m]],
                [units_weight[0], units_weight[0], units_weight[1], units_weight[1]],
                [0, 1, 0, 1],
            )

        return order(run, gate_backs[0][m])

    def branch_project(m):
        def run(first):
            return project(starts, [first, hiddens[1][m]], units_weight, [2, 2])

        return order(run, hiddens[0][m])

    def leave(m, parts):
        back, gain_part = norm_back(middles[m], mlp_factors[m], add_sums(parts))
        middle_grad = upstreams[m] + back
        return (RESIDUAL * middle_grad).astype(BF16), middle_grad, gain_part

    def unit_step(h):
        made = order(lambda a: mlp(a, branch_grads, units_weight[h]), second_all)
        hiddens.append(made[0::3])
        gate_backs.append(made[1::3])
        up_backs.append(made[2::3])
        return [
            (second_all, gate_backs[h]),
            (second_all, up_backs[h]),
            (branch_grads, hiddens[h]),
        ]

    products = unit_step(0)
    unit_grads.append(collect_z(products))
    unit_grads.append(collect_z(unit_step(1)))
    sums = [None, send_sums(back_project(1))]
    sums[0] = send_sums(back_project(0))
    left = [None, order(lambda a: leave(1, a), sums[1])]
    here = [None, send_rows(left[1][0])]
    left[0] = order(lambda a: leave(0, a), sums[0])
    here[0] = send_rows(left[0][0])
    attn_grads = [None, order(join_rows, here[1], starts)]

    def back_attend(m, grad, later):
        queries, pairs, log_total, _, factors = found[m]
        return attend_back(
            m,
            heads,
            m == micro_count - 1,
            work_length,
            grad,
            attn_weight,
            (queries, pairs, log_total, factors),
            tables,
            found[0][1] if m else None,
            later,
        )

    def normed_project(back):
        return project(starts, [back], [attn_weight], [0])

    def end(m, parts):
        back, gain_part = norm_back(streams[m], attn_factors[m], add_sums(parts))
        return left[m][1] + back, gain_part

    def finish(m, parts):
        return valids[m] * (middles[m] + RESIDUAL * add_sums(parts))

    back1, scaled1, later = order(lambda a: back_attend(1, a, None), attn_grads[1])
    sums[1] = send_sums(order(normed_project, back1))
    attn_grads[0] = order(join_rows, here[0], starts)
    unit_parts = [trade(order(lambda a: a, unit_grads[0]))]
    back0, scaled0 = order(lambda a: back_attend(0, a, later), attn_grads[0])
    sums[0] = send_sums(order(normed_project, back0))
    unit_parts[0] = order(lambda a: a, unit_parts[0])
    branch = [None, send_sums(branch_project(1))]
    branch[0] = send_sums(branch_project(0))
    grad_attn = collect_z(
        [(tokens_all, [scaled0, scaled1]), (attn_grads, [found[0][3], found[1][3]])]
    )
    ended = [None, order(lambda a: end(1, a), sums[1])]
    ended[0] = order(lambda a: end(0, a), sums[0])
    attn_gain_total = ended[0][1] + ended[1][1]
    mlp_gain_total = left[0][2] + left[1][2]
    input_parts = [ended[0][0], ended[1][0]]
    both = jnp.stack([attn_gain_total, mlp_gain_total], 0)

    def halve(both, bit, swap):
        n = both.shape[1] // 2
        keep = lax.dynamic_slice_in_dim(both, bit * n, n, 1)
        send = lax.dynamic_slice_in_dim(both, (1 - bit) * n, n, 1)
        return order(lambda a: keep + a, swap(send))

    step = hi_count // 2
    while step >= 1:
        both = halve(both, (z // step) % 2, lambda v, s=step: swap_z(v, s, hi_count))
        step //= 2
    for bit, axis in ((x, "lo"), (y, "y"), (c, "core")):
        both = halve(both, bit, lambda v, a=axis: lax.ppermute(v, a, [(0, 1), (1, 0)]))
    n = both.shape[1]
    gains_here = jnp.stack([gain_attn, gain_mlp], 0).astype(F32)

    both = order(lambda a: a / lax.dynamic_slice_in_dim(gains_here, t * n, n, 1), both)
    outputs = [None, order(lambda a: finish(1, a), branch[1])]
    outputs[0] = order(lambda a: finish(0, a), branch[0])

    unit_parts.append(trade(order(lambda a: a, unit_grads[1])))
    u = unit_parts[0].shape[1] // 3

    def units(k):
        return jnp.concatenate([part[:, k * u : (k + 1) * u] for part in unit_parts], 1).astype(F32)

    unit_outs = order(
        lambda a: (units(0) * a, units(1) * a, jnp.transpose(units(2))), mlp_column
    )
    attn_part = trade(order(lambda a: a, grad_attn)).astype(F32)
    qkv_part = attn_part[:, : groups * side] * attn_column

    def columns(first, last):
        return jnp.concatenate(
            [qkv_part[:, g * side + first : g * side + last] for g in range(groups)], 1
        )

    return (
        jnp.stack(outputs, 0)[None],
        jnp.stack(input_parts, 0)[None],
        columns(0, q_width),
        columns(q_width, q_width + HEAD_DIM),
        columns(q_width + HEAD_DIM, side),
        jnp.transpose(attn_part[:, groups * side :]),
        *unit_outs,
        both[0],
        both[1],
    )


def solution(mesh):
    fsdp_count, tensor_count = mesh.shape["fsdp"], mesh.shape["tensor"]
    split = Mesh(
        mesh.devices.reshape(fsdp_count // 2, 2, tensor_count // 2, 2),
        ("hi", "lo", "y", "core"),
    )
    fsdp = ("hi", "lo")
    tensor = ("y", "core")
    rows = P(fsdp, None, tensor, None)
    inward = P(fsdp, tensor)
    outward = P(tensor, fsdp)
    whole = P(("hi", "lo", "y", "core"))
    weights = (inward, inward, inward, outward, inward, inward, outward)
    return jax.shard_map(
        shards,
        mesh=split,
        in_specs=(rows, P(fsdp)) + weights + (P(fsdp), P(fsdp), rows),
        out_specs=(rows, rows) + weights + (whole, whole),
        check_vma=False,
    )
```

```python
import functools

import jax
import jax.numpy as jnp
from jax import lax
from jax.experimental import pallas as pl
from jax.experimental.pallas import tpu as pltpu
from jax.sharding import Mesh, PartitionSpec as P

HEAD_DIM = 64
EPS = 1e-05
MULT = 0.015625
RESIDUAL = 0.22
THETA = 10000000.0
NEGATIVE = -1e30
F32 = jnp.float32
BF16 = jnp.bfloat16
BLOCK = 256
VMEM_LIMIT = 56 * 1024 * 1024
SMEM = pltpu.SMEM


def nn(a, b):
    return lax.dot_general(a, b, (((1,), (0,)), ((), ())), preferred_element_type=F32)


def nt(a, b):
    return lax.dot_general(a, b, (((1,), (1,)), ((), ())), preferred_element_type=F32)


def tn(a, b):
    return lax.dot_general(a, b, (((0,), (0,)), ((), ())), preferred_element_type=F32)


def params():
    return pltpu.CompilerParams(vmem_limit_bytes=VMEM_LIMIT)


def hops(sources, place):
    pairs = []
    for x in range(2):
        for y in range(2):
            for c in range(2):
                if sources != ("same" if x == c else "other"):
                    continue
                px, py, pc = place(x, y, c)
                pairs.append((x * 4 + y * 2 + c, px * 4 + py * 2 + pc))
    return pairs


def over_x(x, y, c):
    return 1 - x, y, c


def over_y(x, y, c):
    return x, 1 - y, c


def over_core(x, y, c):
    return x, y, 1 - c


def flip(pairs):
    return [pair[::-1] for pair in pairs]


FIRST = hops("other", lambda x, y, c: (c, y, x)) + hops("same", over_y)
SECOND = hops("same", over_x) + hops("other", lambda x, y, c: (x, 1 - y, 1 - c))
THIRD = hops("other", over_core)
PASS_Y = hops("other", over_y)
PASS_X = hops("same", over_x)


def send(values, pairs):
    return lax.ppermute(values, ("lo", "y", "core"), pairs)


def trade(values):
    received = send(values, hops("other", lambda x, y, c: (c, y, x)))
    return jnp.where(is_same(), values, received)


def is_same():
    return lax.axis_index("lo") == lax.axis_index("core")


def after(value, anchor):
    return lax.optimization_barrier((value, anchor))[0]


def send_rows(piece):
    first = send(piece, FIRST)
    second = send(piece, SECOND)
    third = send(piece, THIRD)
    return [first, second, third, send(first, PASS_Y), piece, send(first, PASS_X)]


def assemble_kernel(starts, *refs):
    pieces, out, sems = refs[:6], refs[6], refs[7]
    rows = pieces[0].shape[0]

    def copy(piece, k):
        start = pl.multiple_of(starts[k], rows)
        return pltpu.make_async_copy(pieces[piece], out.at[pl.ds(start, rows)], sems.at[k])

    copy(0, 0).start()
    copy(1, 1).start()

    @pl.when(starts[4] == 1)
    def _():
        copy(2, 2).start()
        copy(4, 3).start()

    @pl.when(starts[4] != 1)
    def _():
        copy(3, 2).start()
        copy(5, 3).start()

    for k in range(4):
        copy(k, k).wait()


def join_rows(pieces, starts):
    rows, width = pieces[0].shape
    return pl.pallas_call(
        assemble_kernel,
        out_shape=jax.ShapeDtypeStruct((4 * rows, width), pieces[0].dtype),
        in_specs=[pl.BlockSpec(memory_space=SMEM)] + [pl.BlockSpec(memory_space=pl.ANY)] * 6,
        out_specs=pl.BlockSpec(memory_space=pltpu.VMEM),
        scratch_shapes=[pltpu.SemaphoreType.DMA((4,))],
        compiler_params=params(),
        name="assemble",
    )(starts, *pieces)


def send_sums(parts):
    across_y = send(parts[2], flip(PASS_Y))
    across_x = send(parts[3], flip(PASS_X))
    second = send(parts[1], flip(SECOND))
    third = send(parts[2], flip(THIRD))
    passed = jnp.where(is_same(), across_x, across_y).astype(F32)
    first = send((parts[0].astype(F32) + passed).astype(BF16), flip(FIRST))
    return [first, second, jnp.where(is_same(), parts[3], third)]


def add_sums(parts):
    return sum(part.astype(F32) for part in parts)


def swap_z(values, step, count):
    return lax.ppermute(values, "hi", [(i, i ^ step) for i in range(count)])


class Order:

    def __init__(self):
        self.last = None

    def __call__(self, step, first, *rest):
        if self.last is not None:
            first = after(first, self.last)
        found = step(first, *rest)
        self.last = jax.tree.leaves(found)[0]
        return found


def project_kernel(pairs, rows, starts, *refs):
    lhs, rhs = refs[:pairs], refs[pairs : 2 * pairs]
    outs, total = refs[2 * pairs : -1], refs[-1]
    value = None
    for a, b in zip(lhs, rhs):
        term = nt(a[...], b[...])
        value = term if value is None else value + term
    total[...] = value
    for k, out in enumerate(outs):
        start = pl.multiple_of(starts[k], rows)
        out[...] = total[pl.ds(start, rows), :].astype(BF16)


def project(starts, lhs, rhs, places):
    tall = lhs[0].shape[0]
    count = 4
    rows = tall // count
    wide = rhs[0].shape[0]
    step = min(512, wide)

    def still(j):
        return (0, 0)

    def columns(size, place):
        return pl.BlockSpec((step, size), lambda j: (j, place))

    return pl.pallas_call(
        functools.partial(project_kernel, len(lhs), rows),
        grid=(wide // step,),
        out_shape=(jax.ShapeDtypeStruct((rows, wide), BF16),) * count,
        in_specs=[pl.BlockSpec(memory_space=SMEM)]
        + [pl.BlockSpec(a.shape, still) for a in lhs]
        + [columns(a.shape[1], place) for a, place in zip(lhs, places)],
        out_specs=(pl.BlockSpec((rows, step), lambda j: (0, j)),) * count,
        scratch_shapes=[pltpu.VMEM((tall, step), F32)],
        compiler_params=params(),
        name="project",
    )(starts, *lhs, *rhs)


def mlp_kernel(count, *refs):
    seconds, branch_grads = refs[:count], refs[count : 2 * count]
    w_gate, w_up, w_down = refs[2 * count : 2 * count + 3]
    outs = refs[2 * count + 3 :]
    for m in range(count):
        hidden, gate_back, up_back = outs[3 * m : 3 * m + 3]
        seen = seconds[m][...]
        gate = nn(seen, w_gate[...])
        up = nn(seen, w_up[...])
        grad = nn(branch_grads[m][...], w_down[...])
        sigma = 1.0 / (1.0 + jnp.exp(-gate))
        silu = gate * sigma
        hidden[...] = (silu * up).astype(BF16)
        up_back[...] = (grad * silu).astype(BF16)
        gate_back[...] = (grad * up * (sigma + silu * (1.0 - sigma))).astype(BF16)


def mlp(seconds, branch_grads, weight):
    count = len(seconds)
    tall, width = seconds[0].shape
    units = weight.shape[1] // 3
    step = min(256, units)
    steps = units // step
    whole = pl.BlockSpec((tall, width), lambda j: (0, 0), pipeline_mode=pl.Buffered(1))
    part = pl.BlockSpec((tall, step), lambda j: (0, j))
    shape = jax.ShapeDtypeStruct((tall, units), BF16)
    return pl.pallas_call(
        functools.partial(mlp_kernel, count),
        grid=(steps,),
        out_shape=(shape,) * (3 * count),
        in_specs=[whole] * (2 * count)
        + [
            pl.BlockSpec((width, step), lambda j, k=k: (0, k * steps + j)) for k in range(3)
        ],
        out_specs=(part,) * (3 * count),
        compiler_params=params(),
        name="mlp",
    )(*seconds, *branch_grads, weight, weight, weight)


def grads_kernel(plan, *refs):
    out = refs[-1]
    start = 0
    for pairs in plan:
        value = None
        for a, b in pairs:
            term = tn(refs[a][...], refs[b][...])
            value = term if value is None else value + term
        value = value.astype(BF16).reshape(out.shape[0], out.shape[1], value.shape[1])
        out[:, :, start : start + value.shape[2]] = value
        start += value.shape[2]


def weight_grads(products, count):
    arrays = []
    specs = []
    plan = []
    side = 0
    slab = products[0][0][0].shape[1] // count
    step = max(slab, 256)

    def place(array, cut):
        for i, known in enumerate(arrays):
            if known is array:
                return i
        tall, wide = array.shape
        if cut:
            specs.append(pl.BlockSpec((tall, step), lambda j: (0, j)))
        else:
            specs.append(
                pl.BlockSpec((tall, wide), lambda j: (0, 0), pipeline_mode=pl.Buffered(1))
            )
        arrays.append(array)
        return len(arrays) - 1

    for lhs, rhs in products:
        plan.append([(place(a, True), place(b, False)) for a, b in zip(lhs, rhs)])
        side += rhs[0].shape[1]
    return pl.pallas_call(
        functools.partial(grads_kernel, plan),
        grid=(count * slab // step,),
        out_shape=jax.ShapeDtypeStruct((count, slab, side), BF16),
        in_specs=specs,
        out_specs=pl.BlockSpec((step // slab, slab, side), lambda j: (j, 0, 0)),
        compiler_params=params(),
        name="grads",
    )(*arrays)


def turn(values, cosines, sines):
    lane = lax.broadcasted_iota(jnp.int32, values.shape, 1)
    other = jnp.where(
        lane % HEAD_DIM < HEAD_DIM // 2,
        pltpu.roll(values, 128 - HEAD_DIM // 2, 1),
        pltpu.roll(values, HEAD_DIM // 2, 1),
    )
    return values * cosines + other * sines


def head_block(values, head, high):
    tile = values[:, (head // 2) * 128 : (head // 2 + 1) * 128]
    if (head % 2 == 1) != high:
        tile = pltpu.roll(tile, HEAD_DIM, 1)
    lane = lax.broadcasted_iota(jnp.int32, tile.shape, 1)
    inside = (lane >= HEAD_DIM) if high else (lane < HEAD_DIM)
    return jnp.where(inside, tile, 0.0)


def bias_of(m, rows, j, length):
    seen = m * rows + (j + 1) * BLOCK
    first = m * rows if m else seen - BLOCK
    key = first + lax.broadcasted_iota(jnp.int32, (seen - first, BLOCK), 0)
    query = m * rows + j * BLOCK + lax.broadcasted_iota(jnp.int32, (seen - first, BLOCK), 1)
    return first, seen, jnp.where((key <= query) & (key < length), 0.0, NEGATIVE)


def scores_of(keys, query, bias, first, seen):
    scores = nt(keys[:seen], query)
    if first == 0:
        return scores + bias
    return jnp.concatenate([scores[:first], scores[first:] + bias], 0)


def forward_kernel(m, heads, lengths, *refs):
    tokens, weight, cos_q, sin_q, cos_k, sin_k = refs[:6]
    refs = refs[6:]
    if m:
        before, refs = refs[0], refs[1:]
    queries, pairs, log_total, mixed, factors, flipped = refs
    rows = tokens.shape[0]
    length = lengths[0]
    wide = tokens[...].astype(F32)
    factor = lax.rsqrt(jnp.mean(wide * wide, -1, keepdims=True) + EPS)
    factors[...] = jnp.broadcast_to(factor, (rows, 128))
    qkv = nn(tokens[...], weight[...]) * factor
    parts = []
    for i in range(heads // 2):
        parts.append(turn(qkv[:, i * 128 : (i + 1) * 128], cos_q[...], sin_q[...]))
    query = jnp.concatenate(parts, 1).astype(BF16).astype(F32) * MULT
    queries[...] = query.astype(BF16)
    pair = turn(qkv[:, heads * HEAD_DIM :], cos_k[...], sin_k[...]).astype(BF16)
    pairs[...] = pair
    if m:
        pair = jnp.concatenate([before[...], pair], 0)
    upright = jnp.transpose(pair.astype(F32)).astype(BF16)[HEAD_DIM:]
    for j in range(rows // BLOCK):
        first, seen, bias = bias_of(m, rows, j, length)
        here = slice(j * BLOCK, (j + 1) * BLOCK)
        for h in range(heads):
            q = head_block(query[here], h, False).astype(BF16)
            scores = scores_of(pair, q, bias, first, seen)
            top = jnp.max(scores, 0, keepdims=True)
            expd = jnp.exp(scores - top)
            total = jnp.sum(expd, 0, keepdims=True)
            log_total[0, h : h + 1, here] = top + jnp.log(total)
            out = nn(upright[:, :seen], expd.astype(BF16)) / total
            flipped[h * HEAD_DIM : (h + 1) * HEAD_DIM, here] = out
    mixed[...] = jnp.transpose(flipped[...]).astype(BF16)


def attend(m, heads, lengths, tokens, weight, tables, before):
    rows, width = tokens.shape
    q_width = heads * HEAD_DIM
    groups = weight.shape[1] // (2 * q_width + 128)

    def block(lanes):
        return pl.BlockSpec((rows, lanes), lambda g: (0, g))

    def whole(lanes, place=0):
        return pl.BlockSpec((rows, lanes), lambda g: (place, 0))

    return pl.pallas_call(
        functools.partial(forward_kernel, m, heads),
        grid=(groups,),
        out_shape=(
            jax.ShapeDtypeStruct((rows, groups * q_width), BF16),
            jax.ShapeDtypeStruct((rows, groups * 128), BF16),
            jax.ShapeDtypeStruct((groups, heads, rows), F32),
            jax.ShapeDtypeStruct((rows, groups * q_width), BF16),
            jax.ShapeDtypeStruct((rows, 128), F32),
        ),
        in_specs=[
            pl.BlockSpec(memory_space=SMEM),
            whole(width),
            pl.BlockSpec((width, q_width + 128), lambda g: (0, g)),
        ]
        + [whole(128, m)] * 4
        + ([block(128)] if m else []),
        out_specs=(
            block(q_width),
            block(128),
            pl.BlockSpec((1, heads, rows), lambda g: (g, 0, 0)),
            block(q_width),
            whole(128),
        ),
        scratch_shapes=[pltpu.VMEM((q_width, rows), F32)],
        compiler_params=params(),
        name="attend",
    )(lengths, tokens, weight, *tables, *([before] if m else []))


def backward_kernel(m, heads, last, lengths, *refs):
    grad, w_out, queries, pairs, log_total, factors = refs[:6]
    cos_q, sin_q, cos_k, sin_k = refs[6:10]
    refs = refs[10:]
    if m:
        before, refs = refs[0], refs[1:]
    if not last:
        later, refs = refs[0], refs[1:]
    back, scaled_back, refs = refs[0], refs[1], refs[2:]
    if m:
        earlier, refs = refs[0], refs[1:]
    flipped, pair_grad = refs
    rows = grad.shape[0]
    q_width = heads * HEAD_DIM
    length = lengths[0]
    mixed_grad = nn(grad[...], w_out[...]).astype(BF16).astype(F32)
    query = queries[...].astype(F32)
    pair = pairs[...]
    if m:
        pair = jnp.concatenate([before[...], pair], 0)
    upright = jnp.transpose(pair.astype(F32)).astype(BF16)[:HEAD_DIM]
    pair_grad[...] = jnp.zeros_like(pair_grad)
    if not last:
        pair_grad[m * rows :, :] = later[...]
    for j in range(rows // BLOCK):
        first, seen, bias = bias_of(m, rows, j, length)
        here = slice(j * BLOCK, (j + 1) * BLOCK)
        for h in range(heads):
            q = head_block(query[here], h, False).astype(BF16)
            g = head_block(mixed_grad[here], h, True).astype(BF16)
            scores = scores_of(pair, q, bias, first, seen)
            probs = jnp.exp(scores - log_total[0, h : h + 1, here])
            prob_grad = nt(pair[:seen], g)
            inner = jnp.sum(probs * prob_grad, 0, keepdims=True)
            score_grad = (probs * (prob_grad - inner)).astype(BF16)
            pair_grad[:seen, :] += nn(score_grad, q) + nn(probs.astype(BF16), g)
            flipped[h * HEAD_DIM : (h + 1) * HEAD_DIM, here] = nn(upright[:, :seen], score_grad)
    query_grad = jnp.transpose(flipped[...]) * MULT
    parts = []
    for i in range(heads // 2):
        parts.append(turn(query_grad[:, i * 128 : (i + 1) * 128], cos_q[...], -sin_q[...]))
    parts.append(turn(pair_grad[m * rows :, :], cos_k[...], -sin_k[...]))
    found = jnp.concatenate(parts, 1).astype(BF16)
    back[...] = found
    scaled_back[...] = (found.astype(F32) * factors[:, :1]).astype(BF16)
    if m:
        earlier[...] = pair_grad[: m * rows, :]


def attend_back(m, heads, last, lengths, grad, weight, kept, tables, before, later):
    rows, width = grad.shape
    q_width = heads * HEAD_DIM
    side = q_width + 128
    queries, pairs, log_total, factors = kept
    groups = queries.shape[1] // q_width
    first = groups * side // q_width

    def block(lanes):
        return pl.BlockSpec((rows, lanes), lambda g: (0, g))

    def whole(lanes, place=0):
        return pl.BlockSpec((rows, lanes), lambda g: (place, 0))

    back = jax.ShapeDtypeStruct((rows, groups * side), BF16)
    earlier = (jax.ShapeDtypeStruct((rows, groups * 128), F32),) if m else ()
    return pl.pallas_call(
        functools.partial(backward_kernel, m, heads, last),
        grid=(groups,),
        out_shape=(back, back) + earlier,
        in_specs=[
            pl.BlockSpec(memory_space=SMEM),
            whole(width),
            pl.BlockSpec((width, q_width), lambda g: (0, first + g)),
            block(q_width),
            block(128),
            pl.BlockSpec((1, heads, rows), lambda g: (g, 0, 0)),
            whole(128),
        ]
        + [whole(128, m)] * 4
        + ([block(128)] if m else [])
        + ([] if last else [block(128)]),
        out_specs=(block(side),) * 2 + ((block(128),) if m else ()),
        scratch_shapes=[
            pltpu.VMEM((q_width, rows), F32),
            pltpu.VMEM(((m + 1) * rows, 128), F32),
        ],
        compiler_params=params(),
        name="attend_back",
    )(
        lengths,
        grad,
        weight,
        queries,
        pairs,
        log_total,
        factors,
        *tables,
        *([before] if m else []),
        *([] if last else [later]),
    )


def norm_back(values, factor, weighted):
    scaled = values * factor
    product = weighted * scaled
    back = factor * (weighted - scaled * jnp.mean(product, -1, keepdims=True))
    return back, jnp.sum(product, 0)


def shards(
    tokens,
    lengths,
    w_query,
    w_key,
    w_value,
    w_out,
    w_gate,
    w_up,
    w_down,
    gain_attn,
    gain_mlp,
    cotangent,
):
    hi_count = lax.axis_size("hi")
    slabs = hi_count * 2
    z = lax.axis_index("hi")
    x = lax.axis_index("lo")
    y = lax.axis_index("y")
    c = lax.axis_index("core")
    t = y * 2 + c
    micro_count = tokens.shape[1]
    rows = tokens.shape[2]
    query_rows = rows * 4
    total_rows = micro_count * query_rows
    depth = w_query.shape[0]
    width = depth * slabs
    groups = w_key.shape[1] // HEAD_DIM
    heads = w_query.shape[1] // HEAD_DIM // groups
    q_width = heads * HEAD_DIM
    side = q_width + 128
    attn_column = gain_attn.astype(F32)[:, None]
    mlp_column = gain_mlp.astype(F32)[:, None]

    near = [y * 2 + x, y * 2 + 1 - x]
    far = [(1 - y) * 2 + x, (1 - y) * 2 + 1 - x]
    same = (x == c).astype(jnp.int32)
    starts = jnp.where(
        x == c,
        jnp.stack([far[0], far[1], near[1], near[0]]),
        jnp.stack([near[0], near[1], far[0], far[1]]),
    )
    starts = jnp.append(starts * rows, same).astype(jnp.int32)
    length = lengths[0]
    work_length = trade(lengths)

    order = Order()

    def gather_z(piece):
        return lax.all_gather(piece, ("hi", "core"), axis=0, tiled=True)

    def collect_z(products):
        lhs, rhs = products[0]

        def run(first):
            return weight_grads([(lhs, [first] + list(rhs[1:]))] + products[1:], slabs)

        total = order(run, rhs[0])
        return lax.psum_scatter(total, ("hi", "core"), scatter_dimension=0, tiled=False)

    def scaled(weight, column):
        return (weight.astype(F32) * column).astype(BF16)

    out_turned = jnp.transpose(w_out)
    down_turned = jnp.transpose(w_down)

    def attention_columns():
        parts = []
        for g in range(groups):
            parts.append(w_query[:, g * q_width : (g + 1) * q_width])
            parts.append(w_key[:, g * HEAD_DIM : (g + 1) * HEAD_DIM])
            parts.append(w_value[:, g * HEAD_DIM : (g + 1) * HEAD_DIM])
        return jnp.concatenate([scaled(jnp.concatenate(parts, 1), attn_column), out_turned], 1)

    def unit_columns(h):
        n = w_gate.shape[1] // 2
        here = slice(h * n, (h + 1) * n)
        return jnp.concatenate(
            [
                scaled(w_gate[:, here], mlp_column),
                scaled(w_up[:, here], mlp_column),
                down_turned[:, here],
            ],
            1,
        )

    half_dim = HEAD_DIM // 2
    freqs = jnp.exp(-jnp.log(THETA) * jnp.arange(half_dim).astype(F32) / half_dim)
    angles = jnp.arange(total_rows).astype(F32)[:, None] * freqs[None, :]
    cosines, sines = jnp.cos(angles), jnp.sin(angles)
    cos_head = jnp.concatenate([cosines, cosines], 1)
    sin_head = jnp.concatenate([-sines, sines], 1)
    tables = (
        jnp.concatenate([cos_head, cos_head], 1),
        jnp.concatenate([sin_head, sin_head], 1),
        jnp.concatenate([cos_head, jnp.ones_like(cos_head)], 1),
        jnp.concatenate([sin_head, jnp.zeros_like(sin_head)], 1),
    )

    valids = []
    upstreams = []
    streams = []
    attn_factors = []
    for m in range(micro_count):
        place = m * query_rows + t * rows + jnp.arange(rows)
        valid = (place < length).astype(F32)[:, None]
        valids.append(valid)
        upstreams.append(valid * cotangent[0, m].astype(F32))
        stream = tokens[0, m].astype(F32)
        streams.append(stream)
        attn_factors.append(lax.rsqrt(jnp.mean(stream * stream, -1, keepdims=True) + EPS))

    attn_piece = trade(after(attention_columns(), work_length))
    attn_weight = gather_z(attn_piece)
    here = [send_rows(after(tokens[0, 0], attn_piece))]
    units_piece = [trade(after(unit_columns(0), attn_piece))]
    tokens_all = [order(join_rows, here[0], starts)]
    here.append(send_rows(after(tokens[0, 1], attn_piece)))
    units_weight = [gather_z(order(lambda a: a, units_piece[0]))]

    def forward(m, rows_all):
        return attend(
            m, heads, work_length, rows_all, attn_weight, tables, found[0][1] if m else None
        )

    out_columns = attn_weight[:, groups * side :]

    def out_project(mixed):
        return project(starts, [mixed], [out_columns], [0])

    def enter(m, parts):
        middle = streams[m] + RESIDUAL * add_sums(parts)
        factor = lax.rsqrt(jnp.mean(middle * middle, -1, keepdims=True) + EPS)
        return (middle * factor).astype(BF16), middle, factor

    found = [order(lambda a: forward(0, a), tokens_all[0])]
    sums = [send_sums(order(out_project, found[0][3]))]
    tokens_all.append(order(join_rows, here[1], starts))
    branch_rows = [(RESIDUAL * upstreams[m]).astype(BF16) for m in range(micro_count)]
    branch = [send_rows(after(branch_rows[0], tokens_all[0]))]
    branch.append(send_rows(after(branch_rows[1], found[0][0])))
    branch_grads = [order(join_rows, branch[0], starts)]
    units_piece.append(trade(after(unit_columns(1), found[0][0])))
    found.append(order(lambda a: forward(1, a), tokens_all[1]))
    sums.append(send_sums(order(out_project, found[1][3])))
    entered = [order(lambda a: enter(0, a), sums[0])]
    here = [send_rows(entered[0][0])]
    branch_grads.append(order(join_rows, branch[1], starts))
    units_weight.append(gather_z(order(lambda a: a, units_piece[1])))
    second_all = [order(join_rows, here[0], starts)]
    entered.append(order(lambda a: enter(1, a), sums[1]))
    here.append(send_rows(entered[1][0]))
    second_all.append(order(join_rows, here[1], starts))
    middles = [e[1] for e in entered]
    mlp_factors = [e[2] for e in entered]

    hiddens, gate_backs, up_backs, unit_grads = [], [], [], []
    def back_project(m):
        def run(first):
            return project(
                starts,
                [first, up_backs[0][m], gate_backs[1][m], up_backs[1][m]],
                [units_weight[0], units_weight[0], units_weight[1], units_weight[1]],
                [0, 1, 0, 1],
            )

        return order(run, gate_backs[0][m])

    def branch_project(m):
        def run(first):
            return project(starts, [first, hiddens[1][m]], units_weight, [2, 2])

        return order(run, hiddens[0][m])

    def leave(m, parts):
        back, gain_part = norm_back(middles[m], mlp_factors[m], add_sums(parts))
        middle_grad = upstreams[m] + back
        return (RESIDUAL * middle_grad).astype(BF16), middle_grad, gain_part

    def unit_step(h):
        made = order(lambda a: mlp(a, branch_grads, units_weight[h]), second_all)
        hiddens.append(made[0::3])
        gate_backs.append(made[1::3])
        up_backs.append(made[2::3])
        return [
            (second_all, gate_backs[h]),
            (second_all, up_backs[h]),
            (branch_grads, hiddens[h]),
        ]

    products = unit_step(0)
    unit_grads.append(collect_z(products))
    unit_grads.append(collect_z(unit_step(1)))
    sums = [None, send_sums(back_project(1))]
    sums[0] = send_sums(back_project(0))
    branch = [None, send_sums(branch_project(1))]
    branch[0] = send_sums(branch_project(0))
    left = [None, order(lambda a: leave(1, a), sums[1])]
    here = [None, send_rows(left[1][0])]
    left[0] = order(lambda a: leave(0, a), sums[0])
    here[0] = send_rows(left[0][0])
    attn_grads = [None, order(join_rows, here[1], starts)]

    def back_attend(m, grad, later):
        queries, pairs, log_total, _, factors = found[m]
        return attend_back(
            m,
            heads,
            m == micro_count - 1,
            work_length,
            grad,
            attn_weight,
            (queries, pairs, log_total, factors),
            tables,
            found[0][1] if m else None,
            later,
        )

    def normed_project(back):
        return project(starts, [back], [attn_weight], [0])

    def end(m, parts):
        back, gain_part = norm_back(streams[m], attn_factors[m], add_sums(parts))
        return left[m][1] + back, gain_part

    def finish(m, parts):
        return valids[m] * (middles[m] + RESIDUAL * add_sums(parts))

    back1, scaled1, later = order(lambda a: back_attend(1, a, None), attn_grads[1])
    sums[1] = send_sums(order(normed_project, back1))
    attn_grads[0] = order(join_rows, here[0], starts)
    outputs = [None, order(lambda a: finish(1, a), branch[1])]
    unit_parts = [trade(order(lambda a: a, unit_grads[0]))]
    back0, scaled0 = order(lambda a: back_attend(0, a, later), attn_grads[0])
    sums[0] = send_sums(order(normed_project, back0))
    outputs[0] = order(lambda a: finish(0, a), branch[0])
    unit_parts[0] = order(lambda a: a, unit_parts[0])
    grad_attn = collect_z(
        [(tokens_all, [scaled0, scaled1]), (attn_grads, [found[0][3], found[1][3]])]
    )
    unit_parts.append(trade(order(lambda a: a, unit_grads[1])))
    ended = [None, order(lambda a: end(1, a), sums[1])]
    ended[0] = order(lambda a: end(0, a), sums[0])
    unit_parts[1] = order(lambda a: a, unit_parts[1])
    attn_gain_total = ended[0][1] + ended[1][1]
    mlp_gain_total = left[0][2] + left[1][2]
    input_parts = [ended[0][0], ended[1][0]]
    both = jnp.stack([attn_gain_total, mlp_gain_total], 0)

    def halve(both, bit, swap):
        n = both.shape[1] // 2
        keep = lax.dynamic_slice_in_dim(both, bit * n, n, 1)
        send = lax.dynamic_slice_in_dim(both, (1 - bit) * n, n, 1)
        return order(lambda a: keep + a, swap(send))

    step = hi_count // 2
    while step >= 1:
        both = halve(both, (z // step) % 2, lambda v, s=step: swap_z(v, s, hi_count))
        step //= 2
    for bit, axis in ((x, "lo"), (y, "y"), (c, "core")):
        both = halve(both, bit, lambda v, a=axis: lax.ppermute(v, a, [(0, 1), (1, 0)]))
    n = both.shape[1]
    gains_here = jnp.stack([gain_attn, gain_mlp], 0).astype(F32)

    both = order(lambda a: a / lax.dynamic_slice_in_dim(gains_here, t * n, n, 1), both)

    u = unit_parts[0].shape[1] // 3

    def units(k):
        return jnp.concatenate([part[:, k * u : (k + 1) * u] for part in unit_parts], 1).astype(F32)

    unit_outs = order(
        lambda a: (units(0) * a, units(1) * a, jnp.transpose(units(2))), mlp_column
    )
    attn_part = trade(order(lambda a: a, grad_attn)).astype(F32)
    qkv_part = attn_part[:, : groups * side] * attn_column

    def columns(first, last):
        return jnp.concatenate(
            [qkv_part[:, g * side + first : g * side + last] for g in range(groups)], 1
        )

    return (
        jnp.stack(outputs, 0)[None],
        jnp.stack(input_parts, 0)[None],
        columns(0, q_width),
        columns(q_width, q_width + HEAD_DIM),
        columns(q_width + HEAD_DIM, side),
        jnp.transpose(attn_part[:, groups * side :]),
        *unit_outs,
        both[0],
        both[1],
    )


def solution(mesh):
    fsdp_count, tensor_count = mesh.shape["fsdp"], mesh.shape["tensor"]
    split = Mesh(
        mesh.devices.reshape(fsdp_count // 2, 2, tensor_count // 2, 2),
        ("hi", "lo", "y", "core"),
    )
    fsdp = ("hi", "lo")
    tensor = ("y", "core")
    rows = P(fsdp, None, tensor, None)
    inward = P(fsdp, tensor)
    outward = P(tensor, fsdp)
    whole = P(("hi", "lo", "y", "core"))
    weights = (inward, inward, inward, outward, inward, inward, outward)
    return jax.shard_map(
        shards,
        mesh=split,
        in_specs=(rows, P(fsdp)) + weights + (P(fsdp), P(fsdp), rows),
        out_specs=(rows, rows) + weights + (whole, whole),
        check_vma=False,
    )
```

```python
import functools

import jax
import jax.numpy as jnp
from jax import lax
from jax.experimental import pallas as pl
from jax.experimental.pallas import tpu as pltpu
from jax.sharding import Mesh, PartitionSpec as P

HEAD_DIM = 64
EPS = 1e-05
MULT = 0.015625
RESIDUAL = 0.22
THETA = 10000000.0
NEGATIVE = -1e30
F32 = jnp.float32
BF16 = jnp.bfloat16
BLOCK = 256
VMEM_LIMIT = 56 * 1024 * 1024
SMEM = pltpu.SMEM


def nn(a, b):
    return lax.dot_general(a, b, (((1,), (0,)), ((), ())), preferred_element_type=F32)


def nt(a, b):
    return lax.dot_general(a, b, (((1,), (1,)), ((), ())), preferred_element_type=F32)


def tn(a, b):
    return lax.dot_general(a, b, (((0,), (0,)), ((), ())), preferred_element_type=F32)


def params():
    return pltpu.CompilerParams(vmem_limit_bytes=VMEM_LIMIT)


def hops(sources, place):
    pairs = []
    for x in range(2):
        for y in range(2):
            for c in range(2):
                if sources != ("same" if x == c else "other"):
                    continue
                px, py, pc = place(x, y, c)
                pairs.append((x * 4 + y * 2 + c, px * 4 + py * 2 + pc))
    return pairs


def over_x(x, y, c):
    return 1 - x, y, c


def over_y(x, y, c):
    return x, 1 - y, c


def over_core(x, y, c):
    return x, y, 1 - c


def flip(pairs):
    return [pair[::-1] for pair in pairs]


FIRST = hops("other", lambda x, y, c: (c, y, x)) + hops("same", over_y)
SECOND = hops("same", over_x) + hops("other", lambda x, y, c: (x, 1 - y, 1 - c))
THIRD = hops("other", over_core)
PASS_Y = hops("other", over_y)
PASS_X = hops("same", over_x)


def send(values, pairs):
    return lax.ppermute(values, ("lo", "y", "core"), pairs)


def trade(values):
    received = send(values, hops("other", lambda x, y, c: (c, y, x)))
    return jnp.where(is_same(), values, received)


def is_same():
    return lax.axis_index("lo") == lax.axis_index("core")


def after(value, anchor):
    return lax.optimization_barrier((value, anchor))[0]


def send_rows(piece):
    first = send(piece, FIRST)
    second = send(piece, SECOND)
    third = send(piece, THIRD)
    return [first, second, third, send(first, PASS_Y), piece, send(first, PASS_X)]


def assemble_kernel(starts, *refs):
    pieces, out, sems = refs[:6], refs[6], refs[7]
    rows = pieces[0].shape[0]

    def copy(piece, k):
        start = pl.multiple_of(starts[k], rows)
        return pltpu.make_async_copy(pieces[piece], out.at[pl.ds(start, rows)], sems.at[k])

    copy(0, 0).start()
    copy(1, 1).start()

    @pl.when(starts[4] == 1)
    def _():
        copy(2, 2).start()
        copy(4, 3).start()

    @pl.when(starts[4] != 1)
    def _():
        copy(3, 2).start()
        copy(5, 3).start()

    for k in range(4):
        copy(k, k).wait()


def join_rows(pieces, starts):
    rows, width = pieces[0].shape
    return pl.pallas_call(
        assemble_kernel,
        out_shape=jax.ShapeDtypeStruct((4 * rows, width), pieces[0].dtype),
        in_specs=[pl.BlockSpec(memory_space=SMEM)] + [pl.BlockSpec(memory_space=pl.ANY)] * 6,
        out_specs=pl.BlockSpec(memory_space=pltpu.VMEM),
        scratch_shapes=[pltpu.SemaphoreType.DMA((4,))],
        compiler_params=params(),
        name="assemble",
    )(starts, *pieces)


def send_sums(parts):
    across_y = send(parts[2], flip(PASS_Y))
    across_x = send(parts[3], flip(PASS_X))
    second = send(parts[1], flip(SECOND))
    third = send(parts[2], flip(THIRD))
    passed = jnp.where(is_same(), across_x, across_y).astype(F32)
    first = send((parts[0].astype(F32) + passed).astype(BF16), flip(FIRST))
    return [first, second, jnp.where(is_same(), parts[3], third)]


def add_sums(parts):
    return sum(part.astype(F32) for part in parts)


def swap_z(values, step, count):
    return lax.ppermute(values, "hi", [(i, i ^ step) for i in range(count)])


class Order:

    def __init__(self):
        self.last = None

    def __call__(self, step, first, *rest):
        if self.last is not None:
            first = after(first, self.last)
        found = step(first, *rest)
        self.last = jax.tree.leaves(found)[0]
        return found


def project_kernel(pairs, rows, starts, *refs):
    lhs, rhs = refs[:pairs], refs[pairs : 2 * pairs]
    outs, total = refs[2 * pairs : -1], refs[-1]
    value = None
    for a, b in zip(lhs, rhs):
        term = nt(a[...], b[...])
        value = term if value is None else value + term
    total[...] = value
    for k, out in enumerate(outs):
        start = pl.multiple_of(starts[k], rows)
        out[...] = total[pl.ds(start, rows), :].astype(BF16)


def project(starts, lhs, rhs, places):
    tall = lhs[0].shape[0]
    count = 4
    rows = tall // count
    wide = rhs[0].shape[0]
    step = min(512, wide)

    def still(j):
        return (0, 0)

    def columns(size, place):
        return pl.BlockSpec((step, size), lambda j: (j, place))

    return pl.pallas_call(
        functools.partial(project_kernel, len(lhs), rows),
        grid=(wide // step,),
        out_shape=(jax.ShapeDtypeStruct((rows, wide), BF16),) * count,
        in_specs=[pl.BlockSpec(memory_space=SMEM)]
        + [pl.BlockSpec(a.shape, still) for a in lhs]
        + [columns(a.shape[1], place) for a, place in zip(lhs, places)],
        out_specs=(pl.BlockSpec((rows, step), lambda j: (0, j)),) * count,
        scratch_shapes=[pltpu.VMEM((tall, step), F32)],
        compiler_params=params(),
        name="project",
    )(starts, *lhs, *rhs)


def mlp_kernel(count, *refs):
    seconds, branch_grads = refs[:count], refs[count : 2 * count]
    w_gate, w_up, w_down = refs[2 * count : 2 * count + 3]
    outs = refs[2 * count + 3 :]
    for m in range(count):
        hidden, gate_back, up_back = outs[3 * m : 3 * m + 3]
        seen = seconds[m][...]
        gate = nn(seen, w_gate[...])
        up = nn(seen, w_up[...])
        grad = nn(branch_grads[m][...], w_down[...])
        sigma = 1.0 / (1.0 + jnp.exp(-gate))
        silu = gate * sigma
        hidden[...] = (silu * up).astype(BF16)
        up_back[...] = (grad * silu).astype(BF16)
        gate_back[...] = (grad * up * (sigma + silu * (1.0 - sigma))).astype(BF16)


def mlp(seconds, branch_grads, weight):
    count = len(seconds)
    tall, width = seconds[0].shape
    units = weight.shape[1] // 3
    step = min(256, units)
    steps = units // step
    whole = pl.BlockSpec((tall, width), lambda j: (0, 0), pipeline_mode=pl.Buffered(1))
    part = pl.BlockSpec((tall, step), lambda j: (0, j))
    shape = jax.ShapeDtypeStruct((tall, units), BF16)
    return pl.pallas_call(
        functools.partial(mlp_kernel, count),
        grid=(steps,),
        out_shape=(shape,) * (3 * count),
        in_specs=[whole] * (2 * count)
        + [
            pl.BlockSpec((width, step), lambda j, k=k: (0, k * steps + j)) for k in range(3)
        ],
        out_specs=(part,) * (3 * count),
        compiler_params=params(),
        name="mlp",
    )(*seconds, *branch_grads, weight, weight, weight)


def grads_kernel(plan, *refs):
    out = refs[-1]
    start = 0
    for pairs in plan:
        value = None
        for a, b in pairs:
            term = tn(refs[a][...], refs[b][...])
            value = term if value is None else value + term
        value = value.astype(BF16).reshape(out.shape[0], out.shape[1], value.shape[1])
        out[:, :, start : start + value.shape[2]] = value
        start += value.shape[2]


def weight_grads(products, count):
    arrays = []
    specs = []
    plan = []
    side = 0
    slab = products[0][0][0].shape[1] // count
    step = max(slab, 256)

    def place(array, cut):
        for i, known in enumerate(arrays):
            if known is array:
                return i
        tall, wide = array.shape
        if cut:
            specs.append(pl.BlockSpec((tall, step), lambda j: (0, j)))
        else:
            specs.append(
                pl.BlockSpec((tall, wide), lambda j: (0, 0), pipeline_mode=pl.Buffered(1))
            )
        arrays.append(array)
        return len(arrays) - 1

    for lhs, rhs in products:
        plan.append([(place(a, True), place(b, False)) for a, b in zip(lhs, rhs)])
        side += rhs[0].shape[1]
    return pl.pallas_call(
        functools.partial(grads_kernel, plan),
        grid=(count * slab // step,),
        out_shape=jax.ShapeDtypeStruct((count, slab, side), BF16),
        in_specs=specs,
        out_specs=pl.BlockSpec((step // slab, slab, side), lambda j: (j, 0, 0)),
        compiler_params=params(),
        name="grads",
    )(*arrays)


def turn(values, cosines, sines):
    lane = lax.broadcasted_iota(jnp.int32, values.shape, 1)
    other = jnp.where(
        lane % HEAD_DIM < HEAD_DIM // 2,
        pltpu.roll(values, 128 - HEAD_DIM // 2, 1),
        pltpu.roll(values, HEAD_DIM // 2, 1),
    )
    return values * cosines + other * sines


def head_block(values, head, high):
    tile = values[:, (head // 2) * 128 : (head // 2 + 1) * 128]
    if (head % 2 == 1) != high:
        tile = pltpu.roll(tile, HEAD_DIM, 1)
    lane = lax.broadcasted_iota(jnp.int32, tile.shape, 1)
    inside = (lane >= HEAD_DIM) if high else (lane < HEAD_DIM)
    return jnp.where(inside, tile, 0.0)


def bias_of(m, rows, j, length):
    seen = m * rows + (j + 1) * BLOCK
    first = m * rows if m else seen - BLOCK
    key = first + lax.broadcasted_iota(jnp.int32, (seen - first, BLOCK), 0)
    query = m * rows + j * BLOCK + lax.broadcasted_iota(jnp.int32, (seen - first, BLOCK), 1)
    return first, seen, jnp.where((key <= query) & (key < length), 0.0, NEGATIVE)


def scores_of(keys, query, bias, first, seen):
    scores = nt(keys[:seen], query)
    if first == 0:
        return scores + bias
    return jnp.concatenate([scores[:first], scores[first:] + bias], 0)


def forward_kernel(m, heads, lengths, *refs):
    tokens, weight, cos_q, sin_q, cos_k, sin_k = refs[:6]
    refs = refs[6:]
    if m:
        before, refs = refs[0], refs[1:]
    queries, pairs, log_total, mixed, factors, flipped = refs
    rows = tokens.shape[0]
    length = lengths[0]
    wide = tokens[...].astype(F32)
    factor = lax.rsqrt(jnp.mean(wide * wide, -1, keepdims=True) + EPS)
    factors[...] = jnp.broadcast_to(factor, (rows, 128))
    qkv = nn(tokens[...], weight[...]) * factor
    parts = []
    for i in range(heads // 2):
        parts.append(turn(qkv[:, i * 128 : (i + 1) * 128], cos_q[...], sin_q[...]))
    query = jnp.concatenate(parts, 1).astype(BF16).astype(F32) * MULT
    queries[...] = query.astype(BF16)
    pair = turn(qkv[:, heads * HEAD_DIM :], cos_k[...], sin_k[...]).astype(BF16)
    pairs[...] = pair
    if m:
        pair = jnp.concatenate([before[...], pair], 0)
    upright = jnp.transpose(pair.astype(F32)).astype(BF16)[HEAD_DIM:]
    for j in range(rows // BLOCK):
        first, seen, bias = bias_of(m, rows, j, length)
        here = slice(j * BLOCK, (j + 1) * BLOCK)
        for h in range(heads):
            q = head_block(query[here], h, False).astype(BF16)
            scores = scores_of(pair, q, bias, first, seen)
            top = jnp.max(scores, 0, keepdims=True)
            expd = jnp.exp(scores - top)
            total = jnp.sum(expd, 0, keepdims=True)
            log_total[0, h : h + 1, here] = top + jnp.log(total)
            out = nn(upright[:, :seen], expd.astype(BF16)) / total
            flipped[h * HEAD_DIM : (h + 1) * HEAD_DIM, here] = out
    mixed[...] = jnp.transpose(flipped[...]).astype(BF16)


def attend(m, heads, lengths, tokens, weight, tables, before):
    rows, width = tokens.shape
    q_width = heads * HEAD_DIM
    groups = weight.shape[1] // (2 * q_width + 128)

    def block(lanes):
        return pl.BlockSpec((rows, lanes), lambda g: (0, g))

    def whole(lanes, place=0):
        return pl.BlockSpec((rows, lanes), lambda g: (place, 0))

    return pl.pallas_call(
        functools.partial(forward_kernel, m, heads),
        grid=(groups,),
        out_shape=(
            jax.ShapeDtypeStruct((rows, groups * q_width), BF16),
            jax.ShapeDtypeStruct((rows, groups * 128), BF16),
            jax.ShapeDtypeStruct((groups, heads, rows), F32),
            jax.ShapeDtypeStruct((rows, groups * q_width), BF16),
            jax.ShapeDtypeStruct((rows, 128), F32),
        ),
        in_specs=[
            pl.BlockSpec(memory_space=SMEM),
            whole(width),
            pl.BlockSpec((width, q_width + 128), lambda g: (0, g)),
        ]
        + [whole(128, m)] * 4
        + ([block(128)] if m else []),
        out_specs=(
            block(q_width),
            block(128),
            pl.BlockSpec((1, heads, rows), lambda g: (g, 0, 0)),
            block(q_width),
            whole(128),
        ),
        scratch_shapes=[pltpu.VMEM((q_width, rows), F32)],
        compiler_params=params(),
        name="attend",
    )(lengths, tokens, weight, *tables, *([before] if m else []))


def backward_kernel(m, heads, last, lengths, *refs):
    grad, w_out, queries, pairs, log_total, factors = refs[:6]
    cos_q, sin_q, cos_k, sin_k = refs[6:10]
    refs = refs[10:]
    if m:
        before, refs = refs[0], refs[1:]
    if not last:
        later, refs = refs[0], refs[1:]
    back, scaled_back, refs = refs[0], refs[1], refs[2:]
    if m:
        earlier, refs = refs[0], refs[1:]
    flipped, pair_grad = refs
    rows = grad.shape[0]
    q_width = heads * HEAD_DIM
    length = lengths[0]
    mixed_grad = nn(grad[...], w_out[...]).astype(BF16).astype(F32)
    query = queries[...].astype(F32)
    pair = pairs[...]
    if m:
        pair = jnp.concatenate([before[...], pair], 0)
    upright = jnp.transpose(pair.astype(F32)).astype(BF16)[:HEAD_DIM]
    pair_grad[...] = jnp.zeros_like(pair_grad)
    if not last:
        pair_grad[m * rows :, :] = later[...]
    for j in range(rows // BLOCK):
        first, seen, bias = bias_of(m, rows, j, length)
        here = slice(j * BLOCK, (j + 1) * BLOCK)
        for h in range(heads):
            q = head_block(query[here], h, False).astype(BF16)
            g = head_block(mixed_grad[here], h, True).astype(BF16)
            scores = scores_of(pair, q, bias, first, seen)
            probs = jnp.exp(scores - log_total[0, h : h + 1, here])
            prob_grad = nt(pair[:seen], g)
            inner = jnp.sum(probs * prob_grad, 0, keepdims=True)
            score_grad = (probs * (prob_grad - inner)).astype(BF16)
            pair_grad[:seen, :] += nn(score_grad, q) + nn(probs.astype(BF16), g)
            flipped[h * HEAD_DIM : (h + 1) * HEAD_DIM, here] = nn(upright[:, :seen], score_grad)
    query_grad = jnp.transpose(flipped[...]) * MULT
    parts = []
    for i in range(heads // 2):
        parts.append(turn(query_grad[:, i * 128 : (i + 1) * 128], cos_q[...], -sin_q[...]))
    parts.append(turn(pair_grad[m * rows :, :], cos_k[...], -sin_k[...]))
    found = jnp.concatenate(parts, 1).astype(BF16)
    back[...] = found
    scaled_back[...] = (found.astype(F32) * factors[:, :1]).astype(BF16)
    if m:
        earlier[...] = pair_grad[: m * rows, :]


def attend_back(m, heads, last, lengths, grad, weight, kept, tables, before, later):
    rows, width = grad.shape
    q_width = heads * HEAD_DIM
    side = q_width + 128
    queries, pairs, log_total, factors = kept
    groups = queries.shape[1] // q_width
    first = groups * side // q_width

    def block(lanes):
        return pl.BlockSpec((rows, lanes), lambda g: (0, g))

    def whole(lanes, place=0):
        return pl.BlockSpec((rows, lanes), lambda g: (place, 0))

    back = jax.ShapeDtypeStruct((rows, groups * side), BF16)
    earlier = (jax.ShapeDtypeStruct((rows, groups * 128), F32),) if m else ()
    return pl.pallas_call(
        functools.partial(backward_kernel, m, heads, last),
        grid=(groups,),
        out_shape=(back, back) + earlier,
        in_specs=[
            pl.BlockSpec(memory_space=SMEM),
            whole(width),
            pl.BlockSpec((width, q_width), lambda g: (0, first + g)),
            block(q_width),
            block(128),
            pl.BlockSpec((1, heads, rows), lambda g: (g, 0, 0)),
            whole(128),
        ]
        + [whole(128, m)] * 4
        + ([block(128)] if m else [])
        + ([] if last else [block(128)]),
        out_specs=(block(side),) * 2 + ((block(128),) if m else ()),
        scratch_shapes=[
            pltpu.VMEM((q_width, rows), F32),
            pltpu.VMEM(((m + 1) * rows, 128), F32),
        ],
        compiler_params=params(),
        name="attend_back",
    )(
        lengths,
        grad,
        weight,
        queries,
        pairs,
        log_total,
        factors,
        *tables,
        *([before] if m else []),
        *([] if last else [later]),
    )


def norm_back(values, factor, weighted):
    scaled = values * factor
    product = weighted * scaled
    back = factor * (weighted - scaled * jnp.mean(product, -1, keepdims=True))
    return back, jnp.sum(product, 0)


def shards(
    tokens,
    lengths,
    w_query,
    w_key,
    w_value,
    w_out,
    w_gate,
    w_up,
    w_down,
    gain_attn,
    gain_mlp,
    cotangent,
):
    hi_count = lax.axis_size("hi")
    slabs = hi_count * 2
    z = lax.axis_index("hi")
    x = lax.axis_index("lo")
    y = lax.axis_index("y")
    c = lax.axis_index("core")
    t = y * 2 + c
    micro_count = tokens.shape[1]
    rows = tokens.shape[2]
    query_rows = rows * 4
    total_rows = micro_count * query_rows
    depth = w_query.shape[0]
    width = depth * slabs
    groups = w_key.shape[1] // HEAD_DIM
    heads = w_query.shape[1] // HEAD_DIM // groups
    q_width = heads * HEAD_DIM
    side = q_width + 128
    attn_column = gain_attn.astype(F32)[:, None]
    mlp_column = gain_mlp.astype(F32)[:, None]

    near = [y * 2 + x, y * 2 + 1 - x]
    far = [(1 - y) * 2 + x, (1 - y) * 2 + 1 - x]
    same = (x == c).astype(jnp.int32)
    starts = jnp.where(
        x == c,
        jnp.stack([far[0], far[1], near[1], near[0]]),
        jnp.stack([near[0], near[1], far[0], far[1]]),
    )
    starts = jnp.append(starts * rows, same).astype(jnp.int32)
    length = lengths[0]
    work_length = trade(lengths)

    order = Order()

    def gather_z(piece):
        return lax.all_gather(piece, ("hi", "core"), axis=0, tiled=True)

    def collect_z(products):
        lhs, rhs = products[0]

        def run(first):
            return weight_grads([(lhs, [first] + list(rhs[1:]))] + products[1:], slabs)

        total = order(run, rhs[0])
        return lax.psum_scatter(total, ("hi", "core"), scatter_dimension=0, tiled=False)

    def scaled(weight, column):
        return (weight.astype(F32) * column).astype(BF16)

    out_turned = jnp.transpose(w_out)
    down_turned = jnp.transpose(w_down)

    def attention_columns():
        parts = []
        for g in range(groups):
            parts.append(w_query[:, g * q_width : (g + 1) * q_width])
            parts.append(w_key[:, g * HEAD_DIM : (g + 1) * HEAD_DIM])
            parts.append(w_value[:, g * HEAD_DIM : (g + 1) * HEAD_DIM])
        return jnp.concatenate([scaled(jnp.concatenate(parts, 1), attn_column), out_turned], 1)

    def unit_columns(h):
        n = w_gate.shape[1] // 2
        here = slice(h * n, (h + 1) * n)
        return jnp.concatenate(
            [
                scaled(w_gate[:, here], mlp_column),
                scaled(w_up[:, here], mlp_column),
                down_turned[:, here],
            ],
            1,
        )

    half_dim = HEAD_DIM // 2
    freqs = jnp.exp(-jnp.log(THETA) * jnp.arange(half_dim).astype(F32) / half_dim)
    angles = jnp.arange(total_rows).astype(F32)[:, None] * freqs[None, :]
    cosines, sines = jnp.cos(angles), jnp.sin(angles)
    cos_head = jnp.concatenate([cosines, cosines], 1)
    sin_head = jnp.concatenate([-sines, sines], 1)
    tables = (
        jnp.concatenate([cos_head, cos_head], 1),
        jnp.concatenate([sin_head, sin_head], 1),
        jnp.concatenate([cos_head, jnp.ones_like(cos_head)], 1),
        jnp.concatenate([sin_head, jnp.zeros_like(sin_head)], 1),
    )

    valids = []
    upstreams = []
    streams = []
    attn_factors = []
    for m in range(micro_count):
        place = m * query_rows + t * rows + jnp.arange(rows)
        valid = (place < length).astype(F32)[:, None]
        valids.append(valid)
        upstreams.append(valid * cotangent[0, m].astype(F32))
        stream = tokens[0, m].astype(F32)
        streams.append(stream)
        attn_factors.append(lax.rsqrt(jnp.mean(stream * stream, -1, keepdims=True) + EPS))

    attn_piece = trade(after(attention_columns(), work_length))
    attn_weight = gather_z(attn_piece)
    here = [send_rows(after(tokens[0, 0], attn_piece))]
    units_piece = [trade(after(unit_columns(0), attn_piece))]
    tokens_all = [order(join_rows, here[0], starts)]
    here.append(send_rows(after(tokens[0, 1], attn_piece)))
    units_weight = [gather_z(order(lambda a: a, units_piece[0]))]

    def forward(m, rows_all):
        return attend(
            m, heads, work_length, rows_all, attn_weight, tables, found[0][1] if m else None
        )

    out_columns = attn_weight[:, groups * side :]

    def out_project(mixed):
        return project(starts, [mixed], [out_columns], [0])

    def enter(m, parts):
        middle = streams[m] + RESIDUAL * add_sums(parts)
        factor = lax.rsqrt(jnp.mean(middle * middle, -1, keepdims=True) + EPS)
        return (middle * factor).astype(BF16), middle, factor

    found = [order(lambda a: forward(0, a), tokens_all[0])]
    sums = [send_sums(order(out_project, found[0][3]))]
    tokens_all.append(order(join_rows, here[1], starts))
    branch_rows = [(RESIDUAL * upstreams[m]).astype(BF16) for m in range(micro_count)]
    branch = [send_rows(after(branch_rows[0], tokens_all[0]))]
    branch.append(send_rows(after(branch_rows[1], found[0][0])))
    branch_grads = [order(join_rows, branch[0], starts)]
    units_piece.append(trade(after(unit_columns(1), found[0][0])))
    units_weight.append(gather_z(order(lambda a: a, units_piece[1])))
    found.append(order(lambda a: forward(1, a), tokens_all[1]))
    sums.append(send_sums(order(out_project, found[1][3])))
    entered = [order(lambda a: enter(0, a), sums[0])]
    here = [send_rows(entered[0][0])]
    branch_grads.append(order(join_rows, branch[1], starts))
    second_all = [order(join_rows, here[0], starts)]
    entered.append(order(lambda a: enter(1, a), sums[1]))
    here.append(send_rows(entered[1][0]))
    second_all.append(order(join_rows, here[1], starts))
    middles = [e[1] for e in entered]
    mlp_factors = [e[2] for e in entered]

    hiddens, gate_backs, up_backs, unit_grads = [], [], [], []
    def back_project(m):
        def run(first):
            return project(
                starts,
                [first, up_backs[0][m], gate_backs[1][m], up_backs[1][m]],
                [units_weight[0], units_weight[0], units_weight[1], units_weight[1]],
                [0, 1, 0, 1],
            )

        return order(run, gate_backs[0][m])

    def branch_project(m):
        def run(first):
            return project(starts, [first, hiddens[1][m]], units_weight, [2, 2])

        return order(run, hiddens[0][m])

    def leave(m, parts):
        back, gain_part = norm_back(middles[m], mlp_factors[m], add_sums(parts))
        middle_grad = upstreams[m] + back
        return (RESIDUAL * middle_grad).astype(BF16), middle_grad, gain_part

    def unit_step(h):
        made = order(lambda a: mlp(a, branch_grads, units_weight[h]), second_all)
        hiddens.append(made[0::3])
        gate_backs.append(made[1::3])
        up_backs.append(made[2::3])
        return [
            (second_all, gate_backs[h]),
            (second_all, up_backs[h]),
            (branch_grads, hiddens[h]),
        ]

    products = unit_step(0)
    unit_grads.append(collect_z(products))
    unit_grads.append(collect_z(unit_step(1)))
    sums = [None, send_sums(back_project(1))]
    sums[0] = send_sums(back_project(0))
    branch = [None, send_sums(branch_project(1))]
    branch[0] = send_sums(branch_project(0))
    left = [None, order(lambda a: leave(1, a), sums[1])]
    here = [None, send_rows(left[1][0])]
    left[0] = order(lambda a: leave(0, a), sums[0])
    here[0] = send_rows(left[0][0])
    attn_grads = [None, order(join_rows, here[1], starts)]

    def back_attend(m, grad, later):
        queries, pairs, log_total, _, factors = found[m]
        return attend_back(
            m,
            heads,
            m == micro_count - 1,
            work_length,
            grad,
            attn_weight,
            (queries, pairs, log_total, factors),
            tables,
            found[0][1] if m else None,
            later,
        )

    def normed_project(back):
        return project(starts, [back], [attn_weight], [0])

    def end(m, parts):
        back, gain_part = norm_back(streams[m], attn_factors[m], add_sums(parts))
        return left[m][1] + back, gain_part

    def finish(m, parts):
        return valids[m] * (middles[m] + RESIDUAL * add_sums(parts))

    back1, scaled1, later = order(lambda a: back_attend(1, a, None), attn_grads[1])
    sums[1] = send_sums(order(normed_project, back1))
    attn_grads[0] = order(join_rows, here[0], starts)
    outputs = [None, order(lambda a: finish(1, a), branch[1])]
    unit_parts = [trade(order(lambda a: a, unit_grads[0]))]
    back0, scaled0 = order(lambda a: back_attend(0, a, later), attn_grads[0])
    sums[0] = send_sums(order(normed_project, back0))
    outputs[0] = order(lambda a: finish(0, a), branch[0])
    unit_parts[0] = order(lambda a: a, unit_parts[0])
    grad_attn = collect_z(
        [(tokens_all, [scaled0, scaled1]), (attn_grads, [found[0][3], found[1][3]])]
    )
    unit_parts.append(trade(order(lambda a: a, unit_grads[1])))
    ended = [None, order(lambda a: end(1, a), sums[1])]
    ended[0] = order(lambda a: end(0, a), sums[0])
    unit_parts[1] = order(lambda a: a, unit_parts[1])
    attn_gain_total = ended[0][1] + ended[1][1]
    mlp_gain_total = left[0][2] + left[1][2]
    input_parts = [ended[0][0], ended[1][0]]
    both = jnp.stack([attn_gain_total, mlp_gain_total], 0)

    def halve(both, bit, swap):
        n = both.shape[1] // 2
        keep = lax.dynamic_slice_in_dim(both, bit * n, n, 1)
        send = lax.dynamic_slice_in_dim(both, (1 - bit) * n, n, 1)
        return order(lambda a: keep + a, swap(send))

    step = hi_count // 2
    while step >= 1:
        both = halve(both, (z // step) % 2, lambda v, s=step: swap_z(v, s, hi_count))
        step //= 2
    for bit, axis in ((x, "lo"), (y, "y"), (c, "core")):
        both = halve(both, bit, lambda v, a=axis: lax.ppermute(v, a, [(0, 1), (1, 0)]))
    n = both.shape[1]
    gains_here = jnp.stack([gain_attn, gain_mlp], 0).astype(F32)

    both = order(lambda a: a / lax.dynamic_slice_in_dim(gains_here, t * n, n, 1), both)

    u = unit_parts[0].shape[1] // 3

    def units(k):
        return jnp.concatenate([part[:, k * u : (k + 1) * u] for part in unit_parts], 1).astype(F32)

    unit_outs = order(
        lambda a: (units(0) * a, units(1) * a, jnp.transpose(units(2))), mlp_column
    )
    attn_part = trade(order(lambda a: a, grad_attn)).astype(F32)
    qkv_part = attn_part[:, : groups * side] * attn_column

    def columns(first, last):
        return jnp.concatenate(
            [qkv_part[:, g * side + first : g * side + last] for g in range(groups)], 1
        )

    return (
        jnp.stack(outputs, 0)[None],
        jnp.stack(input_parts, 0)[None],
        columns(0, q_width),
        columns(q_width, q_width + HEAD_DIM),
        columns(q_width + HEAD_DIM, side),
        jnp.transpose(attn_part[:, groups * side :]),
        *unit_outs,
        both[0],
        both[1],
    )


def solution(mesh):
    fsdp_count, tensor_count = mesh.shape["fsdp"], mesh.shape["tensor"]
    split = Mesh(
        mesh.devices.reshape(fsdp_count // 2, 2, tensor_count // 2, 2),
        ("hi", "lo", "y", "core"),
    )
    fsdp = ("hi", "lo")
    tensor = ("y", "core")
    rows = P(fsdp, None, tensor, None)
    inward = P(fsdp, tensor)
    outward = P(tensor, fsdp)
    whole = P(("hi", "lo", "y", "core"))
    weights = (inward, inward, inward, outward, inward, inward, outward)
    return jax.shard_map(
        shards,
        mesh=split,
        in_specs=(rows, P(fsdp)) + weights + (P(fsdp), P(fsdp), rows),
        out_specs=(rows, rows) + weights + (whole, whole),
        check_vma=False,
    )
```

```python
import functools

import jax
import jax.numpy as jnp
from jax import lax
from jax.experimental import pallas as pl
from jax.experimental.pallas import tpu as pltpu
from jax.sharding import Mesh, PartitionSpec as P

HEAD_DIM = 64
EPS = 1e-05
MULT = 0.015625
RESIDUAL = 0.22
THETA = 10000000.0
NEGATIVE = -1e30
F32 = jnp.float32
BF16 = jnp.bfloat16
BLOCK = 256
VMEM_LIMIT = 56 * 1024 * 1024
SMEM = pltpu.SMEM


def nn(a, b):
    return lax.dot_general(a, b, (((1,), (0,)), ((), ())), preferred_element_type=F32)


def nt(a, b):
    return lax.dot_general(a, b, (((1,), (1,)), ((), ())), preferred_element_type=F32)


def tn(a, b):
    return lax.dot_general(a, b, (((0,), (0,)), ((), ())), preferred_element_type=F32)


def params():
    return pltpu.CompilerParams(vmem_limit_bytes=VMEM_LIMIT)


def hops(sources, place):
    pairs = []
    for x in range(2):
        for y in range(2):
            for c in range(2):
                if sources != ("same" if x == c else "other"):
                    continue
                px, py, pc = place(x, y, c)
                pairs.append((x * 4 + y * 2 + c, px * 4 + py * 2 + pc))
    return pairs


def over_x(x, y, c):
    return 1 - x, y, c


def over_y(x, y, c):
    return x, 1 - y, c


def over_core(x, y, c):
    return x, y, 1 - c


def flip(pairs):
    return [pair[::-1] for pair in pairs]


FIRST = hops("other", lambda x, y, c: (c, y, x)) + hops("same", over_y)
SECOND = hops("same", over_x) + hops("other", lambda x, y, c: (x, 1 - y, 1 - c))
THIRD = hops("other", over_core)
PASS_Y = hops("other", over_y)
PASS_X = hops("same", over_x)


def send(values, pairs):
    return lax.ppermute(values, ("lo", "y", "core"), pairs)


def trade(values):
    received = send(values, hops("other", lambda x, y, c: (c, y, x)))
    return jnp.where(is_same(), values, received)


def is_same():
    return lax.axis_index("lo") == lax.axis_index("core")


def after(value, anchor):
    return lax.optimization_barrier((value, anchor))[0]


def send_rows(piece):
    first = send(piece, FIRST)
    second = send(piece, SECOND)
    third = send(piece, THIRD)
    return [first, second, third, send(first, PASS_Y), piece, send(first, PASS_X)]


def assemble_kernel(starts, *refs):
    pieces, out, sems = refs[:6], refs[6], refs[7]
    rows = pieces[0].shape[0]

    def copy(piece, k):
        start = pl.multiple_of(starts[k], rows)
        return pltpu.make_async_copy(pieces[piece], out.at[pl.ds(start, rows)], sems.at[k])

    copy(0, 0).start()
    copy(1, 1).start()

    @pl.when(starts[4] == 1)
    def _():
        copy(2, 2).start()
        copy(4, 3).start()

    @pl.when(starts[4] != 1)
    def _():
        copy(3, 2).start()
        copy(5, 3).start()

    for k in range(4):
        copy(k, k).wait()


def join_rows(pieces, starts):
    rows, width = pieces[0].shape
    return pl.pallas_call(
        assemble_kernel,
        out_shape=jax.ShapeDtypeStruct((4 * rows, width), pieces[0].dtype),
        in_specs=[pl.BlockSpec(memory_space=SMEM)] + [pl.BlockSpec(memory_space=pl.ANY)] * 6,
        out_specs=pl.BlockSpec(memory_space=pltpu.VMEM),
        scratch_shapes=[pltpu.SemaphoreType.DMA((4,))],
        compiler_params=params(),
        name="assemble",
    )(starts, *pieces)


def send_sums(parts):
    across_y = send(parts[2], flip(PASS_Y))
    across_x = send(parts[3], flip(PASS_X))
    second = send(parts[1], flip(SECOND))
    third = send(parts[2], flip(THIRD))
    passed = jnp.where(is_same(), across_x, across_y).astype(F32)
    first = send((parts[0].astype(F32) + passed).astype(BF16), flip(FIRST))
    return [first, second, jnp.where(is_same(), parts[3], third)]


def add_sums(parts):
    return sum(part.astype(F32) for part in parts)


def swap_z(values, step, count):
    return lax.ppermute(values, "hi", [(i, i ^ step) for i in range(count)])


class Order:

    def __init__(self):
        self.last = None

    def __call__(self, step, first, *rest):
        if self.last is not None:
            first = after(first, self.last)
        found = step(first, *rest)
        self.last = jax.tree.leaves(found)[0]
        return found


def project_kernel(pairs, rows, starts, *refs):
    lhs, rhs = refs[:pairs], refs[pairs : 2 * pairs]
    outs, total = refs[2 * pairs : -1], refs[-1]
    value = None
    for a, b in zip(lhs, rhs):
        term = nt(a[...], b[...])
        value = term if value is None else value + term
    total[...] = value
    for k, out in enumerate(outs):
        start = pl.multiple_of(starts[k], rows)
        out[...] = total[pl.ds(start, rows), :].astype(BF16)


def project(starts, lhs, rhs, places):
    tall = lhs[0].shape[0]
    count = 4
    rows = tall // count
    wide = rhs[0].shape[0]
    step = min(512, wide)

    def still(j):
        return (0, 0)

    def columns(size, place):
        return pl.BlockSpec((step, size), lambda j: (j, place))

    return pl.pallas_call(
        functools.partial(project_kernel, len(lhs), rows),
        grid=(wide // step,),
        out_shape=(jax.ShapeDtypeStruct((rows, wide), BF16),) * count,
        in_specs=[pl.BlockSpec(memory_space=SMEM)]
        + [pl.BlockSpec(a.shape, still) for a in lhs]
        + [columns(a.shape[1], place) for a, place in zip(lhs, places)],
        out_specs=(pl.BlockSpec((rows, step), lambda j: (0, j)),) * count,
        scratch_shapes=[pltpu.VMEM((tall, step), F32)],
        compiler_params=params(),
        name="project",
    )(starts, *lhs, *rhs)


def mlp_kernel(count, *refs):
    seconds, branch_grads = refs[:count], refs[count : 2 * count]
    w_gate, w_up, w_down = refs[2 * count : 2 * count + 3]
    outs = refs[2 * count + 3 :]
    for m in range(count):
        hidden, gate_back, up_back = outs[3 * m : 3 * m + 3]
        seen = seconds[m][...]
        gate = nn(seen, w_gate[...])
        up = nn(seen, w_up[...])
        grad = nn(branch_grads[m][...], w_down[...])
        sigma = 1.0 / (1.0 + jnp.exp(-gate))
        silu = gate * sigma
        hidden[...] = (silu * up).astype(BF16)
        up_back[...] = (grad * silu).astype(BF16)
        gate_back[...] = (grad * up * (sigma + silu * (1.0 - sigma))).astype(BF16)


def mlp(seconds, branch_grads, weight):
    count = len(seconds)
    tall, width = seconds[0].shape
    units = weight.shape[1] // 3
    step = min(256, units)
    steps = units // step
    whole = pl.BlockSpec((tall, width), lambda j: (0, 0), pipeline_mode=pl.Buffered(1))
    part = pl.BlockSpec((tall, step), lambda j: (0, j))
    shape = jax.ShapeDtypeStruct((tall, units), BF16)
    return pl.pallas_call(
        functools.partial(mlp_kernel, count),
        grid=(steps,),
        out_shape=(shape,) * (3 * count),
        in_specs=[whole] * (2 * count)
        + [
            pl.BlockSpec((width, step), lambda j, k=k: (0, k * steps + j)) for k in range(3)
        ],
        out_specs=(part,) * (3 * count),
        compiler_params=params(),
        name="mlp",
    )(*seconds, *branch_grads, weight, weight, weight)


def grads_kernel(plan, *refs):
    out = refs[-1]
    start = 0
    for pairs in plan:
        value = None
        for a, b in pairs:
            term = tn(refs[a][...], refs[b][...])
            value = term if value is None else value + term
        value = value.astype(BF16).reshape(out.shape[0], out.shape[1], value.shape[1])
        out[:, :, start : start + value.shape[2]] = value
        start += value.shape[2]


def weight_grads(products, count):
    arrays = []
    specs = []
    plan = []
    side = 0
    slab = products[0][0][0].shape[1] // count
    step = max(slab, 256)

    def place(array, cut):
        for i, known in enumerate(arrays):
            if known is array:
                return i
        tall, wide = array.shape
        if cut:
            specs.append(pl.BlockSpec((tall, step), lambda j: (0, j)))
        else:
            specs.append(
                pl.BlockSpec((tall, wide), lambda j: (0, 0), pipeline_mode=pl.Buffered(1))
            )
        arrays.append(array)
        return len(arrays) - 1

    for lhs, rhs in products:
        plan.append([(place(a, True), place(b, False)) for a, b in zip(lhs, rhs)])
        side += rhs[0].shape[1]
    return pl.pallas_call(
        functools.partial(grads_kernel, plan),
        grid=(count * slab // step,),
        out_shape=jax.ShapeDtypeStruct((count, slab, side), BF16),
        in_specs=specs,
        out_specs=pl.BlockSpec((step // slab, slab, side), lambda j: (j, 0, 0)),
        compiler_params=params(),
        name="grads",
    )(*arrays)


def turn(values, cosines, sines):
    lane = lax.broadcasted_iota(jnp.int32, values.shape, 1)
    other = jnp.where(
        lane % HEAD_DIM < HEAD_DIM // 2,
        pltpu.roll(values, 128 - HEAD_DIM // 2, 1),
        pltpu.roll(values, HEAD_DIM // 2, 1),
    )
    return values * cosines + other * sines


def head_block(values, head, high):
    tile = values[:, (head // 2) * 128 : (head // 2 + 1) * 128]
    if (head % 2 == 1) != high:
        tile = pltpu.roll(tile, HEAD_DIM, 1)
    lane = lax.broadcasted_iota(jnp.int32, tile.shape, 1)
    inside = (lane >= HEAD_DIM) if high else (lane < HEAD_DIM)
    return jnp.where(inside, tile, 0.0)


def bias_of(m, rows, j, length):
    seen = m * rows + (j + 1) * BLOCK
    first = m * rows if m else seen - BLOCK
    key = first + lax.broadcasted_iota(jnp.int32, (seen - first, BLOCK), 0)
    query = m * rows + j * BLOCK + lax.broadcasted_iota(jnp.int32, (seen - first, BLOCK), 1)
    return first, seen, jnp.where((key <= query) & (key < length), 0.0, NEGATIVE)


def scores_of(keys, query, bias, first, seen):
    scores = nt(keys[:seen], query)
    if first == 0:
        return scores + bias
    return jnp.concatenate([scores[:first], scores[first:] + bias], 0)


def forward_kernel(m, heads, lengths, *refs):
    tokens, weight, cos_q, sin_q, cos_k, sin_k = refs[:6]
    refs = refs[6:]
    if m:
        before, refs = refs[0], refs[1:]
    queries, pairs, log_total, mixed, factors, flipped = refs
    rows = tokens.shape[0]
    length = lengths[0]
    wide = tokens[...].astype(F32)
    factor = lax.rsqrt(jnp.mean(wide * wide, -1, keepdims=True) + EPS)
    factors[...] = jnp.broadcast_to(factor, (rows, 128))
    qkv = nn(tokens[...], weight[...]) * factor
    parts = []
    for i in range(heads // 2):
        parts.append(turn(qkv[:, i * 128 : (i + 1) * 128], cos_q[...], sin_q[...]))
    query = jnp.concatenate(parts, 1).astype(BF16).astype(F32) * MULT
    queries[...] = query.astype(BF16)
    pair = turn(qkv[:, heads * HEAD_DIM :], cos_k[...], sin_k[...]).astype(BF16)
    pairs[...] = pair
    if m:
        pair = jnp.concatenate([before[...], pair], 0)
    upright = jnp.transpose(pair.astype(F32)).astype(BF16)[HEAD_DIM:]
    for j in range(rows // BLOCK):
        first, seen, bias = bias_of(m, rows, j, length)
        here = slice(j * BLOCK, (j + 1) * BLOCK)
        for h in range(heads):
            q = head_block(query[here], h, False).astype(BF16)
            scores = scores_of(pair, q, bias, first, seen)
            top = jnp.max(scores, 0, keepdims=True)
            expd = jnp.exp(scores - top)
            total = jnp.sum(expd, 0, keepdims=True)
            log_total[0, h : h + 1, here] = top + jnp.log(total)
            out = nn(upright[:, :seen], expd.astype(BF16)) / total
            flipped[h * HEAD_DIM : (h + 1) * HEAD_DIM, here] = out
    mixed[...] = jnp.transpose(flipped[...]).astype(BF16)


def attend(m, heads, lengths, tokens, weight, tables, before):
    rows, width = tokens.shape
    q_width = heads * HEAD_DIM
    groups = weight.shape[1] // (2 * q_width + 128)

    def block(lanes):
        return pl.BlockSpec((rows, lanes), lambda g: (0, g))

    def whole(lanes, place=0):
        return pl.BlockSpec((rows, lanes), lambda g: (place, 0))

    return pl.pallas_call(
        functools.partial(forward_kernel, m, heads),
        grid=(groups,),
        out_shape=(
            jax.ShapeDtypeStruct((rows, groups * q_width), BF16),
            jax.ShapeDtypeStruct((rows, groups * 128), BF16),
            jax.ShapeDtypeStruct((groups, heads, rows), F32),
            jax.ShapeDtypeStruct((rows, groups * q_width), BF16),
            jax.ShapeDtypeStruct((rows, 128), F32),
        ),
        in_specs=[
            pl.BlockSpec(memory_space=SMEM),
            whole(width),
            pl.BlockSpec((width, q_width + 128), lambda g: (0, g)),
        ]
        + [whole(128, m)] * 4
        + ([block(128)] if m else []),
        out_specs=(
            block(q_width),
            block(128),
            pl.BlockSpec((1, heads, rows), lambda g: (g, 0, 0)),
            block(q_width),
            whole(128),
        ),
        scratch_shapes=[pltpu.VMEM((q_width, rows), F32)],
        compiler_params=params(),
        name="attend",
    )(lengths, tokens, weight, *tables, *([before] if m else []))


def backward_kernel(m, heads, last, lengths, *refs):
    grad, w_out, queries, pairs, log_total, factors = refs[:6]
    cos_q, sin_q, cos_k, sin_k = refs[6:10]
    refs = refs[10:]
    if m:
        before, refs = refs[0], refs[1:]
    if not last:
        later, refs = refs[0], refs[1:]
    back, scaled_back, refs = refs[0], refs[1], refs[2:]
    if m:
        earlier, refs = refs[0], refs[1:]
    flipped, pair_grad = refs
    rows = grad.shape[0]
    q_width = heads * HEAD_DIM
    length = lengths[0]
    mixed_grad = nn(grad[...], w_out[...]).astype(BF16).astype(F32)
    query = queries[...].astype(F32)
    pair = pairs[...]
    if m:
        pair = jnp.concatenate([before[...], pair], 0)
    upright = jnp.transpose(pair.astype(F32)).astype(BF16)[:HEAD_DIM]
    pair_grad[...] = jnp.zeros_like(pair_grad)
    if not last:
        pair_grad[m * rows :, :] = later[...]
    for j in range(rows // BLOCK):
        first, seen, bias = bias_of(m, rows, j, length)
        here = slice(j * BLOCK, (j + 1) * BLOCK)
        for h in range(heads):
            q = head_block(query[here], h, False).astype(BF16)
            g = head_block(mixed_grad[here], h, True).astype(BF16)
            scores = scores_of(pair, q, bias, first, seen)
            probs = jnp.exp(scores - log_total[0, h : h + 1, here])
            prob_grad = nt(pair[:seen], g)
            inner = jnp.sum(probs * prob_grad, 0, keepdims=True)
            score_grad = (probs * (prob_grad - inner)).astype(BF16)
            pair_grad[:seen, :] += nn(score_grad, q) + nn(probs.astype(BF16), g)
            flipped[h * HEAD_DIM : (h + 1) * HEAD_DIM, here] = nn(upright[:, :seen], score_grad)
    query_grad = jnp.transpose(flipped[...]) * MULT
    parts = []
    for i in range(heads // 2):
        parts.append(turn(query_grad[:, i * 128 : (i + 1) * 128], cos_q[...], -sin_q[...]))
    parts.append(turn(pair_grad[m * rows :, :], cos_k[...], -sin_k[...]))
    found = jnp.concatenate(parts, 1).astype(BF16)
    back[...] = found
    scaled_back[...] = (found.astype(F32) * factors[:, :1]).astype(BF16)
    if m:
        earlier[...] = pair_grad[: m * rows, :]


def attend_back(m, heads, last, lengths, grad, weight, kept, tables, before, later):
    rows, width = grad.shape
    q_width = heads * HEAD_DIM
    side = q_width + 128
    queries, pairs, log_total, factors = kept
    groups = queries.shape[1] // q_width
    first = groups * side // q_width

    def block(lanes):
        return pl.BlockSpec((rows, lanes), lambda g: (0, g))

    def whole(lanes, place=0):
        return pl.BlockSpec((rows, lanes), lambda g: (place, 0))

    back = jax.ShapeDtypeStruct((rows, groups * side), BF16)
    earlier = (jax.ShapeDtypeStruct((rows, groups * 128), F32),) if m else ()
    return pl.pallas_call(
        functools.partial(backward_kernel, m, heads, last),
        grid=(groups,),
        out_shape=(back, back) + earlier,
        in_specs=[
            pl.BlockSpec(memory_space=SMEM),
            whole(width),
            pl.BlockSpec((width, q_width), lambda g: (0, first + g)),
            block(q_width),
            block(128),
            pl.BlockSpec((1, heads, rows), lambda g: (g, 0, 0)),
            whole(128),
        ]
        + [whole(128, m)] * 4
        + ([block(128)] if m else [])
        + ([] if last else [block(128)]),
        out_specs=(block(side),) * 2 + ((block(128),) if m else ()),
        scratch_shapes=[
            pltpu.VMEM((q_width, rows), F32),
            pltpu.VMEM(((m + 1) * rows, 128), F32),
        ],
        compiler_params=params(),
        name="attend_back",
    )(
        lengths,
        grad,
        weight,
        queries,
        pairs,
        log_total,
        factors,
        *tables,
        *([before] if m else []),
        *([] if last else [later]),
    )


def norm_back(values, factor, weighted):
    scaled = values * factor
    product = weighted * scaled
    back = factor * (weighted - scaled * jnp.mean(product, -1, keepdims=True))
    return back, jnp.sum(product, 0)


def shards(
    tokens,
    lengths,
    w_query,
    w_key,
    w_value,
    w_out,
    w_gate,
    w_up,
    w_down,
    gain_attn,
    gain_mlp,
    cotangent,
):
    hi_count = lax.axis_size("hi")
    slabs = hi_count * 2
    z = lax.axis_index("hi")
    x = lax.axis_index("lo")
    y = lax.axis_index("y")
    c = lax.axis_index("core")
    t = y * 2 + c
    micro_count = tokens.shape[1]
    rows = tokens.shape[2]
    query_rows = rows * 4
    total_rows = micro_count * query_rows
    depth = w_query.shape[0]
    width = depth * slabs
    groups = w_key.shape[1] // HEAD_DIM
    heads = w_query.shape[1] // HEAD_DIM // groups
    q_width = heads * HEAD_DIM
    side = q_width + 128
    attn_column = gain_attn.astype(F32)[:, None]
    mlp_column = gain_mlp.astype(F32)[:, None]

    near = [y * 2 + x, y * 2 + 1 - x]
    far = [(1 - y) * 2 + x, (1 - y) * 2 + 1 - x]
    same = (x == c).astype(jnp.int32)
    starts = jnp.where(
        x == c,
        jnp.stack([far[0], far[1], near[1], near[0]]),
        jnp.stack([near[0], near[1], far[0], far[1]]),
    )
    starts = jnp.append(starts * rows, same).astype(jnp.int32)
    length = lengths[0]

    order = Order()

    def gather_z(piece):
        return lax.all_gather(piece, ("hi", "core"), axis=0, tiled=True)

    def collect_z(products):
        lhs, rhs = products[0]

        def run(first):
            return weight_grads([(lhs, [first] + list(rhs[1:]))] + products[1:], slabs)

        total = order(run, rhs[0])
        return lax.psum_scatter(total, ("hi", "core"), scatter_dimension=0, tiled=False)

    def scaled(weight, column):
        return (weight.astype(F32) * column).astype(BF16)

    out_turned = jnp.transpose(w_out)
    down_turned = jnp.transpose(w_down)

    def attention_columns():
        parts = []
        for g in range(groups):
            parts.append(w_query[:, g * q_width : (g + 1) * q_width])
            parts.append(w_key[:, g * HEAD_DIM : (g + 1) * HEAD_DIM])
            parts.append(w_value[:, g * HEAD_DIM : (g + 1) * HEAD_DIM])
        return jnp.concatenate([scaled(jnp.concatenate(parts, 1), attn_column), out_turned], 1)

    def unit_columns(h):
        n = w_gate.shape[1] // 2
        here = slice(h * n, (h + 1) * n)
        return jnp.concatenate(
            [
                scaled(w_gate[:, here], mlp_column),
                scaled(w_up[:, here], mlp_column),
                down_turned[:, here],
            ],
            1,
        )

    half_dim = HEAD_DIM // 2
    freqs = jnp.exp(-jnp.log(THETA) * jnp.arange(half_dim).astype(F32) / half_dim)
    angles = jnp.arange(total_rows).astype(F32)[:, None] * freqs[None, :]
    cosines, sines = jnp.cos(angles), jnp.sin(angles)
    cos_head = jnp.concatenate([cosines, cosines], 1)
    sin_head = jnp.concatenate([-sines, sines], 1)
    tables = (
        jnp.concatenate([cos_head, cos_head], 1),
        jnp.concatenate([sin_head, sin_head], 1),
        jnp.concatenate([cos_head, jnp.ones_like(cos_head)], 1),
        jnp.concatenate([sin_head, jnp.zeros_like(sin_head)], 1),
    )

    valids = []
    upstreams = []
    streams = []
    attn_factors = []
    for m in range(micro_count):
        place = m * query_rows + t * rows + jnp.arange(rows)
        valid = (place < length).astype(F32)[:, None]
        valids.append(valid)
        upstreams.append(valid * cotangent[0, m].astype(F32))
        stream = tokens[0, m].astype(F32)
        streams.append(stream)
        attn_factors.append(lax.rsqrt(jnp.mean(stream * stream, -1, keepdims=True) + EPS))

    attn_piece = trade(attention_columns())
    work_length = trade(after(lengths, attn_piece))
    attn_weight = gather_z(attn_piece)
    here = [send_rows(after(tokens[0, 0], attn_piece))]
    units_piece = [trade(after(unit_columns(0), work_length))]
    tokens_all = [order(join_rows, here[0], starts)]
    here.append(send_rows(after(tokens[0, 1], attn_piece)))
    units_weight = [gather_z(order(lambda a: a, units_piece[0]))]

    def forward(m, rows_all):
        return attend(
            m, heads, work_length, rows_all, attn_weight, tables, found[0][1] if m else None
        )

    out_columns = attn_weight[:, groups * side :]

    def out_project(mixed):
        return project(starts, [mixed], [out_columns], [0])

    def enter(m, parts):
        middle = streams[m] + RESIDUAL * add_sums(parts)
        factor = lax.rsqrt(jnp.mean(middle * middle, -1, keepdims=True) + EPS)
        return (middle * factor).astype(BF16), middle, factor

    found = [order(lambda a: forward(0, a), tokens_all[0])]
    sums = [send_sums(order(out_project, found[0][3]))]
    tokens_all.append(order(join_rows, here[1], starts))
    branch_rows = [(RESIDUAL * upstreams[m]).astype(BF16) for m in range(micro_count)]
    branch = [send_rows(after(branch_rows[0], tokens_all[0]))]
    branch.append(send_rows(after(branch_rows[1], found[0][0])))
    branch_grads = [order(join_rows, branch[0], starts)]
    units_piece.append(trade(after(unit_columns(1), found[0][0])))
    units_weight.append(gather_z(order(lambda a: a, units_piece[1])))
    found.append(order(lambda a: forward(1, a), tokens_all[1]))
    sums.append(send_sums(order(out_project, found[1][3])))
    entered = [order(lambda a: enter(0, a), sums[0])]
    here = [send_rows(entered[0][0])]
    branch_grads.append(order(join_rows, branch[1], starts))
    second_all = [order(join_rows, here[0], starts)]
    entered.append(order(lambda a: enter(1, a), sums[1]))
    here.append(send_rows(entered[1][0]))
    second_all.append(order(join_rows, here[1], starts))
    middles = [e[1] for e in entered]
    mlp_factors = [e[2] for e in entered]

    hiddens, gate_backs, up_backs, unit_grads = [], [], [], []
    def back_project(m):
        def run(first):
            return project(
                starts,
                [first, up_backs[0][m], gate_backs[1][m], up_backs[1][m]],
                [units_weight[0], units_weight[0], units_weight[1], units_weight[1]],
                [0, 1, 0, 1],
            )

        return order(run, gate_backs[0][m])

    def branch_project(m):
        def run(first):
            return project(starts, [first, hiddens[1][m]], units_weight, [2, 2])

        return order(run, hiddens[0][m])

    def leave(m, parts):
        back, gain_part = norm_back(middles[m], mlp_factors[m], add_sums(parts))
        middle_grad = upstreams[m] + back
        return (RESIDUAL * middle_grad).astype(BF16), middle_grad, gain_part

    def unit_step(h):
        made = order(lambda a: mlp(a, branch_grads, units_weight[h]), second_all)
        hiddens.append(made[0::3])
        gate_backs.append(made[1::3])
        up_backs.append(made[2::3])
        return [
            (second_all, gate_backs[h]),
            (second_all, up_backs[h]),
            (branch_grads, hiddens[h]),
        ]

    products = unit_step(0)
    unit_grads.append(collect_z(products))
    unit_grads.append(collect_z(unit_step(1)))
    sums = [None, send_sums(back_project(1))]
    sums[0] = send_sums(back_project(0))
    branch = [None, send_sums(branch_project(1))]
    branch[0] = send_sums(branch_project(0))
    left = [None, order(lambda a: leave(1, a), sums[1])]
    here = [None, send_rows(left[1][0])]
    left[0] = order(lambda a: leave(0, a), sums[0])
    here[0] = send_rows(left[0][0])
    attn_grads = [None, order(join_rows, here[1], starts)]

    def back_attend(m, grad, later):
        queries, pairs, log_total, _, factors = found[m]
        return attend_back(
            m,
            heads,
            m == micro_count - 1,
            work_length,
            grad,
            attn_weight,
            (queries, pairs, log_total, factors),
            tables,
            found[0][1] if m else None,
            later,
        )

    def normed_project(back):
        return project(starts, [back], [attn_weight], [0])

    def end(m, parts):
        back, gain_part = norm_back(streams[m], attn_factors[m], add_sums(parts))
        return left[m][1] + back, gain_part

    def finish(m, parts):
        return valids[m] * (middles[m] + RESIDUAL * add_sums(parts))

    back1, scaled1, later = order(lambda a: back_attend(1, a, None), attn_grads[1])
    sums[1] = send_sums(order(normed_project, back1))
    attn_grads[0] = order(join_rows, here[0], starts)
    outputs = [None, order(lambda a: finish(1, a), branch[1])]
    unit_parts = [trade(order(lambda a: a, unit_grads[0]))]
    back0, scaled0 = order(lambda a: back_attend(0, a, later), attn_grads[0])
    sums[0] = send_sums(order(normed_project, back0))
    outputs[0] = order(lambda a: finish(0, a), branch[0])
    unit_parts[0] = order(lambda a: a, unit_parts[0])
    grad_attn = collect_z(
        [(tokens_all, [scaled0, scaled1]), (attn_grads, [found[0][3], found[1][3]])]
    )
    unit_parts.append(trade(order(lambda a: a, unit_grads[1])))
    ended = [None, order(lambda a: end(1, a), sums[1])]
    ended[0] = order(lambda a: end(0, a), sums[0])
    unit_parts[1] = order(lambda a: a, unit_parts[1])
    attn_gain_total = ended[0][1] + ended[1][1]
    mlp_gain_total = left[0][2] + left[1][2]
    input_parts = [ended[0][0], ended[1][0]]
    both = jnp.stack([attn_gain_total, mlp_gain_total], 0)

    def halve(both, bit, swap):
        n = both.shape[1] // 2
        keep = lax.dynamic_slice_in_dim(both, bit * n, n, 1)
        send = lax.dynamic_slice_in_dim(both, (1 - bit) * n, n, 1)
        return order(lambda a: keep + a, swap(send))

    step = hi_count // 2
    while step >= 1:
        both = halve(both, (z // step) % 2, lambda v, s=step: swap_z(v, s, hi_count))
        step //= 2
    for bit, axis in ((x, "lo"), (y, "y"), (c, "core")):
        both = halve(both, bit, lambda v, a=axis: lax.ppermute(v, a, [(0, 1), (1, 0)]))
    n = both.shape[1]
    gains_here = jnp.stack([gain_attn, gain_mlp], 0).astype(F32)

    both = order(lambda a: a / lax.dynamic_slice_in_dim(gains_here, t * n, n, 1), both)

    u = unit_parts[0].shape[1] // 3

    def units(k):
        return jnp.concatenate([part[:, k * u : (k + 1) * u] for part in unit_parts], 1).astype(F32)

    unit_outs = order(
        lambda a: (units(0) * a, units(1) * a, jnp.transpose(units(2))), mlp_column
    )
    attn_part = trade(order(lambda a: a, grad_attn)).astype(F32)
    qkv_part = attn_part[:, : groups * side] * attn_column

    def columns(first, last):
        return jnp.concatenate(
            [qkv_part[:, g * side + first : g * side + last] for g in range(groups)], 1
        )

    return (
        jnp.stack(outputs, 0)[None],
        jnp.stack(input_parts, 0)[None],
        columns(0, q_width),
        columns(q_width, q_width + HEAD_DIM),
        columns(q_width + HEAD_DIM, side),
        jnp.transpose(attn_part[:, groups * side :]),
        *unit_outs,
        both[0],
        both[1],
    )


def solution(mesh):
    fsdp_count, tensor_count = mesh.shape["fsdp"], mesh.shape["tensor"]
    split = Mesh(
        mesh.devices.reshape(fsdp_count // 2, 2, tensor_count // 2, 2),
        ("hi", "lo", "y", "core"),
    )
    fsdp = ("hi", "lo")
    tensor = ("y", "core")
    rows = P(fsdp, None, tensor, None)
    inward = P(fsdp, tensor)
    outward = P(tensor, fsdp)
    whole = P(("hi", "lo", "y", "core"))
    weights = (inward, inward, inward, outward, inward, inward, outward)
    return jax.shard_map(
        shards,
        mesh=split,
        in_specs=(rows, P(fsdp)) + weights + (P(fsdp), P(fsdp), rows),
        out_specs=(rows, rows) + weights + (whole, whole),
        check_vma=False,
    )
```
